256 devices in a mesh: chan: 4 (over y), row: 8 (over z), col: 8 (over x, core).
Axes of the slice: x: 4, y: 4, z: 8, core: 2. Of those that a mesh axis runs over, the one named last changes fastest.
Arguments:
- voltages: bfloat16 [8, 2, 4096, 1024], P(None, None, ('row', 'col'), 'chan'), may hold values from -40 to 40
- sources: bfloat16 [8, 2, 4096, 128], P('chan', None, ('row', 'col')), may hold values from -2.83 to 2.83
- initial_gains: float32 [8, 2, 4096], P('chan', None, ('row', 'col')), may hold values from 0.5 to 1.5
- flags: int32 [2048], P(('row', 'col')), may hold values 0 or 1
- neighbours: int32 [8, 2], replicated, may hold values from 0 to 7, as said below
Outputs:
- gains: float32 [8, 2, 4096], P('chan', None, ('row', 'col'))
- step_change: float32 [8, 4], P('chan')
The draws below stay inside these ranges and needn't reach their ends.
Inputs may be any that keep to these rules, and one draw needn't show every extreme that they name: neighbours[c,0] is one to three channels below c and neighbours[c,1] one to three channels above c, clipped to the band.
All inputs are finite; a program needn't handle non-finite values. No bound on the sum of `flags` on one device may be relied on, other than what follows from the above.
Results may differ from the reference program's by a relative error of at most 0.0003.
Values may be sent and summed in bfloat16 or wider, within the bound.
No kernel may reach another device: no remote copies, remote signals or barrier semaphores. Data moves between devices by JAX's collectives and lax.ppermute only.
A program may use at most 64 MiB of HBM per device.

```python
import math
import jax
import jax.numpy as jnp
from jax import lax

NA = 2048
INPUTS = 4096
NTIME = 1024
SOURCE_COUNT = 128
NCHAN = 8
ITERS = 4


def source_field(key):
    values = jax.random.normal(key, (NCHAN, 2, SOURCE_COUNT, 2 * NA), jnp.float32)
    return jnp.clip(values, -4.0, 4.0) * 0.7071067811865476


def draw_sources(key, part):
    electric_field = source_field(key)
    return jnp.transpose(electric_field, (0, 1, 3, 2)).astype(jnp.bfloat16)


def draw_voltages(key, part):
    electric_field = source_field(key)
    key = jax.random.fold_in(key, 11)
    keys = jax.random.split(key, 5)
    antenna_signal = jax.random.normal(keys[0], (NTIME, NCHAN, 2, SOURCE_COUNT), jnp.float32) * 0.7071067811865476
    sky_real = (jnp.einsum('pzv,zvf->pzf', antenna_signal[:, :, 0], electric_field[:, 0], precision=lax.Precision.HIGHEST) - jnp.einsum('pzv,zvf->pzf', antenna_signal[:, :, 1], electric_field[:, 1], precision=lax.Precision.HIGHEST)) / math.sqrt(SOURCE_COUNT)
    sky_imaginary = (jnp.einsum('pzv,zvf->pzf', antenna_signal[:, :, 0], electric_field[:, 1], precision=lax.Precision.HIGHEST) + jnp.einsum('pzv,zvf->pzf', antenna_signal[:, :, 1], electric_field[:, 0], precision=lax.Precision.HIGHEST)) / math.sqrt(SOURCE_COUNT)
    noise_real = jax.random.normal(keys[1], (NTIME, NCHAN, 2 * NA), jnp.float32) * 0.354
    noise_im = jax.random.normal(keys[2], (NTIME, NCHAN, 2 * NA), jnp.float32) * 0.354
    amplitude = jnp.exp(jax.random.uniform(keys[3], (NCHAN, 2 * NA), jnp.float32, math.log(0.5), math.log(2.0)))
    phase = jax.random.uniform(keys[4], (NCHAN, 2 * NA), jnp.float32, -math.pi, math.pi)
    true_re = amplitude * jnp.cos(phase)
    true_im = amplitude * jnp.sin(phase)
    total_re = sky_real + noise_real
    total_im = sky_imaginary + noise_im
    volt_re = true_re * total_re - true_im * total_im
    volt_im = true_re * total_im + true_im * total_re
    stacked = jnp.stack([volt_re, volt_im], axis=2)
    return jnp.transpose(stacked, (1, 2, 3, 0)).astype(jnp.bfloat16)


def draw_neighbours(key, part):
    key = jax.random.fold_in(key, 23)
    offsets = jax.random.randint(key, (NCHAN, 2), 1, 4)
    chans = jnp.arange(NCHAN, dtype=jnp.int32)[:, None]
    lower = jnp.clip(chans - offsets[:, 0:1], 0, NCHAN - 1)
    upper = jnp.clip(chans + offsets[:, 1:2], 0, NCHAN - 1)
    return jnp.concatenate([lower, upper], axis=1).astype(jnp.int32)


def plant(result, rng, smallest, top_value):
    extent = result.shape
    place = [jax.random.randint(jax.random.fold_in(rng, axis), (), 0, extent[axis]) for axis in range(len(extent))]
    result = result.at[tuple(place)].set(smallest)
    longest = extent.index(max(extent))
    place[longest] = (place[longest] + 1) % extent[longest]
    return result.at[tuple(place)].set(top_value)


def steps_of(stream_key, dims, cuts, smallest, high):
    level = 1.0
    for dim, parts in cuts:
        heights = jax.random.uniform(jax.random.fold_in(jax.random.fold_in(stream_key, 6), dim), (parts,), jnp.float32, smallest / len(cuts), high / len(cuts))
        level = level * jnp.repeat(jnp.exp(heights), dims[dim] // parts).reshape((-1,) + (1,) * (len(dims) - 1 - dim))
    return level


def setup_inputs(seed: int = 0) -> dict:
    seeds = jax.random.split(jax.random.key(seed), 6)
    voltages = draw_voltages(jax.random.fold_in(seeds[5], 71), 0)
    sources = draw_sources(jax.random.fold_in(seeds[5], 71), 0)
    initial_gains = jnp.clip(0.5 + 1.0 * jax.random.uniform(seeds[2], (NCHAN, 2, INPUTS), jnp.float32) ** steps_of(seeds[2], (NCHAN, 2, INPUTS), ((0, 4), (2, 64)), -0.2, 0.2), 0.5, 1.5)
    flags = plant((jax.random.randint(seeds[3], (NA,), 0, 16) < 1).astype(jnp.int32), jax.random.fold_in(seeds[3], 1), 0, 1)
    neighbours = draw_neighbours(jax.random.fold_in(seeds[5], 71), 0)
    return {"voltages": voltages, "sources": sources, "initial_gains": initial_gains, "flags": flags, "neighbours": neighbours}


precise = lax.Precision.HIGHEST


def correlate(first, count):
    first = first.astype(jnp.float32)
    swapped = jnp.stack([first[1], -first[0]], axis=0)
    real_part = jnp.einsum('kps,kqs->pq', first, first, precision=precise) / count
    imag_part = jnp.einsum('kps,kqs->pq', swapped, first, precision=precise) / count
    return real_part, imag_part


def channel_terms(pair):
    volt, source_resp = pair
    vis_re, vis_im = correlate(volt, NTIME)
    model_re, model_im = correlate(source_resp, SOURCE_COUNT)
    offdiag = 1.0 - jnp.eye(volt.shape[1], dtype=jnp.float32)
    prod_re = (vis_re * model_re + vis_im * model_im) * offdiag
    prod_im = (vis_im * model_re - vis_re * model_im) * offdiag
    power = (model_re * model_re + model_im * model_im) * offdiag
    return jnp.stack([prod_re, prod_im, power], axis=0)


def reference(voltages, sources, initial_gains, flags, neighbours):
    terms = lax.map(channel_terms, (voltages, sources))
    prod_re = terms[:, 0]
    prod_im = terms[:, 1]
    power = terms[:, 2]
    weight = jnp.repeat(1.0 - flags.astype(jnp.float32), 2)
    chans = jnp.arange(neighbours.shape[0], dtype=jnp.int32)
    smoother = (0.5 * (chans[:, None] == chans[None, :]).astype(jnp.float32)
                + 0.25 * (neighbours[:, 0:1] == chans[None, :]).astype(jnp.float32)
                + 0.25 * (neighbours[:, 1:2] == chans[None, :]).astype(jnp.float32))
    gain_re = initial_gains[:, 0]
    gain_im = initial_gains[:, 1]
    live = weight > 0.5
    changes = []
    for sweep in range(ITERS):
        weighted_re = weight * gain_re
        weighted_im = weight * gain_im
        num_re = (jnp.einsum('cpq,cq->cp', prod_re, weighted_re, precision=precise)
                  - jnp.einsum('cpq,cq->cp', prod_im, weighted_im, precision=precise))
        num_im = (jnp.einsum('cpq,cq->cp', prod_re, weighted_im, precision=precise)
                  + jnp.einsum('cpq,cq->cp', prod_im, weighted_re, precision=precise))
        denominator = jnp.einsum('cpq,cq->cp', power, weight * (gain_re * gain_re + gain_im * gain_im), precision=precise)
        upd_re = jnp.where(live, 0.5 * (num_re / denominator + gain_re), gain_re)
        upd_im = jnp.where(live, 0.5 * (num_im / denominator + gain_im), gain_im)
        smooth_re = jnp.einsum('cj,jp->cp', smoother, upd_re, precision=precise)
        smooth_im = jnp.einsum('cj,jp->cp', smoother, upd_im, precision=precise)
        delta_sum = jnp.sum(weight * ((smooth_re - gain_re) ** 2 + (smooth_im - gain_im) ** 2), axis=1)
        level_sum = jnp.sum(weight * (smooth_re * smooth_re + smooth_im * smooth_im), axis=1)
        changes.append(delta_sum / (level_sum + 1e-6))
        gain_re = smooth_re
        gain_im = smooth_im
    gains = jnp.stack([gain_re, gain_im], axis=1)
    return gains, jnp.stack(changes, axis=1)
```

```python
import functools

import jax
import jax.numpy as jnp
from jax import lax
from jax.experimental import pallas as pl
from jax.experimental.pallas import tpu as pltpu
from jax.sharding import PartitionSpec as P


ITERS = 4
F32 = jnp.float32
BF16 = jnp.bfloat16
NT = (((1,), (1,)), ((), ()))


def call(kernel, out_shape, smem_count, *operands):
    in_specs = [pl.BlockSpec(memory_space=pltpu.SMEM)] * smem_count + [
        pl.BlockSpec(memory_space=pltpu.VMEM)
    ] * (len(operands) - smem_count)
    return pl.pallas_call(
        kernel,
        out_shape=out_shape,
        in_specs=in_specs,
        out_specs=jax.tree.map(lambda _: pl.BlockSpec(memory_space=pltpu.VMEM), out_shape),
        compiler_params=pltpu.CompilerParams(vmem_limit_bytes=24 * 1024 * 1024),
    )(*operands)


def lanes_merge(first, second):
    lane = lax.broadcasted_iota(jnp.int32, first.shape, first.ndim - 1)
    left = lane < 64
    low = jnp.where(left, first, pltpu.roll(second, 64, first.ndim - 1))
    high = jnp.where(left, pltpu.roll(first, 64, first.ndim - 1), second)
    return low, high


def turn_kernel(place_ref, volt_ref, keep_ref, send_ref):
    core = place_ref[0]
    for chan in range(volt_ref.shape[0]):
        for ref, half in ((keep_ref, core), (send_ref, 1 - core)):
            block = volt_ref[chan, :, pl.ds(pl.multiple_of(half * 128, 128), 128)]
            ref[chan] = block.T


def pack_kernel(place_ref, keep_ref, recv_ref, s0, s1, s2, s3, out_ref):
    core, y_id = place_ref[0], place_ref[1]
    flip = jnp.full((128, 128), core, jnp.int32) == 1
    for chan in range(keep_ref.shape[0]):
        own = keep_ref[chan].astype(F32)
        other = recv_ref[chan].astype(F32)
        low, high = lanes_merge(jnp.where(flip, other, own), jnp.where(flip, own, other))
        out_ref[chan, 0:128, :] = low.astype(BF16)
        out_ref[chan, 128:256, :] = high.astype(BF16)
    for step, ref in enumerate((s0, s1, s2, s3)):
        owner = lax.rem(y_id + 4 - step, 4)
        for b in range(2):
            out_ref[2 * owner + b, 256:400, :] = ref[b]


def lay_kernel(place_ref, big_ref, other_ref, nat_ref, yr_ref, yi_ref, misc_ref):
    core, block = place_ref[0], place_ref[2]
    flip = jnp.full((1, 128), core, jnp.int32) == 1
    for z in range(8):
        mine = pl.ds(pl.multiple_of(z * 128 + core * 64, 64), 64)
        theirs = pl.ds(pl.multiple_of(z * 128 + (1 - core) * 64, 64), 64)
        nat_ref[mine, 0:128] = big_ref[z, 256:320, :]
        nat_ref[mine, 128:256] = big_ref[z, 320:384, :]
        nat_ref[theirs, 0:128] = other_ref[z, 0:64, :]
        nat_ref[theirs, 128:256] = other_ref[z, 64:128, :]
        lanes = slice(z * 128, z * 128 + 128)
        x_re, x_im = big_ref[z, 0:128, :], big_ref[z, 128:256, :]
        yr_ref[0:128, lanes] = x_re
        yi_ref[0:128, lanes] = x_im
        x_re, x_im = x_re.astype(F32), x_im.astype(F32)
        own = big_ref[z, 384:400, :].astype(F32)
        other = other_ref[z, 128:144, :].astype(F32)
        own_gain = own[0:1] + own[1:2] + own[2:3]
        other_gain = other[0:1] + other[1:2] + other[2:3]
        gain_re, gain_im = lanes_merge(
            jnp.where(flip, other_gain, own_gain), jnp.where(flip, own_gain, other_gain)
        )
        weight, _ = lanes_merge(
            jnp.where(flip, other[3:4], own[3:4]), jnp.where(flip, own[3:4], other[3:4])
        )
        misc_ref[0:1, lanes] = gain_re
        misc_ref[1:2, lanes] = gain_im
        misc_ref[2:3, lanes] = weight
        misc_ref[4:5, lanes] = jnp.sum(x_re * x_re + x_im * x_im, axis=0, keepdims=True)
    nat = nat_ref[...]
    row = lax.broadcasted_iota(jnp.int32, (16, 128), 0) + block * 16
    pick = (row == lax.broadcasted_iota(jnp.int32, (16, 128), 1)).astype(BF16)
    yr_ref[128:144, :] = lax.dot_general(
        pick, nat[:, 0:128], NT, preferred_element_type=F32
    ).astype(BF16)
    yi_ref[128:144, :] = lax.dot_general(
        pick, nat[:, 128:256], NT, preferred_element_type=F32
    ).astype(BF16)
    wide = nat.astype(F32)
    square = wide * wide
    hi = square.astype(BF16)
    lo = (square - hi.astype(F32)).astype(BF16)
    ones = jnp.ones((16, 256), BF16)
    alpha = lax.dot_general(ones, hi, NT, preferred_element_type=F32) + lax.dot_general(
        ones, lo, NT, preferred_element_type=F32
    )
    misc_ref[3:4, :] = alpha[0:1]
    misc_ref[5:8, :] = jnp.zeros((3, misc_ref.shape[1]), F32)


def split(value):
    hi = value.astype(BF16)
    return hi, (value - hi.astype(F32)).astype(BF16)


def spread(gain_re, gain_im, weight, nat_ref, yr_ref, yi_ref, m_ref):
    w_re = weight * gain_re
    w_im = weight * gain_im
    w_pow = weight * (gain_re * gain_re + gain_im * gain_im)
    total = None
    for start in range(0, nat_ref.shape[0], 256):
        lanes = slice(start, start + 256)
        row = lax.broadcasted_iota(jnp.int32, (144, 256), 0) < 128
        c_re = jnp.where(row, w_re[:, lanes], w_pow[:, lanes])
        c_im = jnp.where(row, w_im[:, lanes], 0.0)
        y_re = yr_ref[:, lanes].astype(F32)
        y_im = yi_ref[:, lanes].astype(F32)
        re_hi, re_lo = split(y_re * c_re + y_im * c_im)
        im_hi, im_lo = split(y_re * c_im - y_im * c_re)
        left = jnp.concatenate([re_hi, re_lo, im_hi, im_lo], axis=0)
        part = jnp.dot(left, nat_ref[lanes, :], preferred_element_type=F32)
        total = part if total is None else total + part
    re = total[0:144] + total[144:288]
    im = total[288:432] + total[432:576]
    m_ref[:, 0:128] = re[:, 0:128] - im[:, 128:256]
    m_ref[:, 128:256] = re[:, 128:256] + im[:, 0:128]


def first_kernel(misc_ref, nat_ref, yr_ref, yi_ref, gain_ref, m_ref):
    gain_re, gain_im, weight = misc_ref[0:1], misc_ref[1:2], misc_ref[2:3]
    gain_ref[0:1] = gain_re
    gain_ref[1:2] = gain_im
    gain_ref[2:8] = jnp.zeros((6, gain_re.shape[1]), F32)
    spread(gain_re, gain_im, weight, nat_ref, yr_ref, yi_ref, m_ref)


def next_kernel(
    sweep, coef_ref, u0, u1, u2, u3, u4, u5, u6, old_ref, misc_ref, nat_ref, yr_ref, yi_ref, gain_ref, m_ref
):
    smooth = coef_ref[0] * u0[...]
    for index, ref in enumerate((u1, u2, u3, u4, u5, u6)):
        smooth = smooth + coef_ref[index + 1] * ref[...]
    gain_re, gain_im, weight = smooth[0:1], smooth[1:2], misc_ref[2:3]
    diff_re, diff_im = gain_re - old_ref[0:1], gain_im - old_ref[1:2]
    delta = jnp.sum(weight * (diff_re * diff_re + diff_im * diff_im), axis=1, keepdims=True)
    level = jnp.sum(weight * (gain_re * gain_re + gain_im * gain_im), axis=1, keepdims=True)
    lane = lax.broadcasted_iota(jnp.int32, gain_re.shape, 1)
    sums = old_ref[2:3]
    sums = jnp.where(lane == 2 * sweep, delta, sums)
    sums = jnp.where(lane == 2 * sweep + 1, level, sums)
    gain_ref[0:1] = gain_re
    gain_ref[1:2] = gain_im
    gain_ref[2:3] = sums
    gain_ref[3:8] = jnp.zeros((5, gain_re.shape[1]), F32)
    spread(gain_re, gain_im, weight, nat_ref, yr_ref, yi_ref, m_ref)


def collect_kernel(m0, m1, m2, m3, gain_ref, misc_ref, nat_ref, yr_ref, yi_ref, out_ref):
    total = (m0[...] + m1[...]) + (m2[...] + m3[...])
    re, im = total[:, 0:128], total[:, 128:256]
    a_hi, a_lo = split(total)
    b_hi, b_lo = split(jnp.concatenate([im, -re], axis=1))
    left = jnp.concatenate([a_hi, a_lo, b_hi, b_lo], axis=0)
    for start in range(0, nat_ref.shape[0], 256):
        lanes = slice(start, start + 256)
        part = lax.dot_general(left, nat_ref[lanes, :], NT, preferred_element_type=F32)
        z_re = part[0:144] + part[144:288]
        z_im = part[288:432] + part[432:576]
        y_re = yr_ref[:, lanes].astype(F32)
        y_im = yi_ref[:, lanes].astype(F32)
        real = y_re * z_re - y_im * z_im
        imag = y_re * z_im + y_im * z_re
        num_re = jnp.sum(real[0:128], axis=0, keepdims=True)
        num_im = jnp.sum(imag[0:128], axis=0, keepdims=True)
        den = jnp.sum(real[128:144], axis=0, keepdims=True)
        g_re, g_im = gain_ref[0:1, lanes], gain_ref[1:2, lanes]
        weight, alpha, power = (misc_ref[r : r + 1, lanes] for r in (2, 3, 4))
        own = alpha * power * weight
        out_ref[0:1, lanes] = num_re - own * g_re
        out_ref[1:2, lanes] = num_im - own * g_im
        out_ref[2:3, lanes] = den - 0.125 * alpha * alpha * weight * (g_re * g_re + g_im * g_im)
        out_ref[3:4, lanes] = jnp.zeros_like(den)


def updated(n0, n1, n2, n3, gain_ref, misc_ref):
    total = (n0[...] + n1[...]) + (n2[...] + n3[...])
    g_re, g_im = gain_ref[0:1], gain_ref[1:2]
    live = misc_ref[2:3] > 0.5
    den = total[2:3]
    u_re = jnp.where(live, 0.5 * (0.125 * total[0:1] / den + g_re), g_re)
    u_im = jnp.where(live, 0.5 * (0.125 * total[1:2] / den + g_im), g_im)
    return u_re, u_im


def update_kernel(n0, n1, n2, n3, gain_ref, misc_ref, out_ref):
    u_re, u_im = updated(n0, n1, n2, n3, gain_ref, misc_ref)
    out_ref[0:1] = u_re
    out_ref[1:2] = u_im


def last_update_kernel(n0, n1, n2, n3, gain_ref, misc_ref, out_ref):
    u_re, u_im = updated(n0, n1, n2, n3, gain_ref, misc_ref)
    rows = (u_re, u_im, gain_ref[0:1], gain_ref[1:2], gain_ref[2:3])
    for index, value in enumerate(rows):
        for z in range(8):
            piece = value[:, z * 128 : z * 128 + 128]
            for target in range(8):
                out_ref[target, index * 8 + z : index * 8 + z + 1, :] = piece


def finish_kernel(place_ref, coef_ref, all_ref, misc_ref, gains_ref, sums_ref, scratch):
    core, y_id, z_id = place_ref[0], place_ref[1], place_ref[3]
    weight = jnp.concatenate([misc_ref[2:3, z * 128 : z * 128 + 128] for z in range(8)], axis=0)
    lane = lax.broadcasted_iota(jnp.int32, (1, 128), 1)
    flip = jnp.full((1, 128), core, jnp.int32) == 1
    sums_ref[...] = jnp.zeros_like(sums_ref)
    for b in range(2):
        smooth = coef_ref[8 * b] * all_ref[0, 0:16, :]
        for j in range(1, 8):
            smooth = smooth + coef_ref[8 * b + j] * all_ref[j, 0:16, :]
        old = all_ref[2 * y_id + b, 16:32, :]
        diff = smooth - old
        delta = weight * (diff[0:8] * diff[0:8] + diff[8:16] * diff[8:16])
        level = weight * (smooth[0:8] * smooth[0:8] + smooth[8:16] * smooth[8:16])
        delta = jnp.sum(jnp.sum(delta, axis=0, keepdims=True), axis=1, keepdims=True)
        level = jnp.sum(jnp.sum(level, axis=0, keepdims=True), axis=1, keepdims=True)
        sums = all_ref[2 * y_id + b, 32:33, :]
        sums = jnp.where(lane == 2 * ITERS - 2, delta, sums)
        sums_ref[b : b + 1, :] = jnp.where(lane == 2 * ITERS - 1, level, sums)
        scratch[...] = smooth
        for part in range(2):
            row = scratch[pl.ds(part * 8 + z_id, 1), :]
            row = jnp.where(flip, pltpu.roll(row, 64, 1), row)
            gains_ref[b, part : part + 1, :] = row[:, 0:64]


def shards(voltages, sources, initial_gains, flags, neighbours):
    y_id, z_id, col_id = lax.axis_index("chan"), lax.axis_index("row"), lax.axis_index("col")
    core = col_id % 2
    place = jnp.stack([core, y_id, y_id * 2 + core, z_id]).astype(jnp.int32)

    def over_core(value):
        return lax.ppermute(value, "col", [(i, i ^ 1) for i in range(8)])

    def over_x(value):
        return [
            lax.ppermute(value, "col", [(i, (i + 2 * d) % 8) for i in range(8)]) for d in (1, 2, 3)
        ]

    def over_y(value):
        return [lax.ppermute(value, "chan", [(i, (i + d) % 4) for i in range(4)]) for d in (1, 2, 3)]

    def over_z(value):
        return [
            lax.ppermute(
                value,
                ("row", "col"),
                [(z * 8 + c, (z + (d if c % 2 == 0 else -d)) % 8 * 8 + c) for z in range(8) for c in range(8)],
            )
            for d in (1, 2, 3)
        ]

    chans = jnp.arange(8, dtype=jnp.int32)

    def smoother_row(chan):
        near = lax.dynamic_slice_in_dim(neighbours, chan, 1, 0)
        return (
            0.5 * (chan == chans).astype(F32)
            + 0.25 * (near[:, 0] == chans).astype(F32)
            + 0.25 * (near[:, 1] == chans).astype(F32)
        )

    own_row = smoother_row(z_id)
    sign = 1 - 2 * core
    hops = jnp.array([0, 1, 2, 3, -1, -2, -3], jnp.int32)
    coef = own_row[(z_id - sign * hops) % 8]
    final_coef = jnp.concatenate([smoother_row(2 * y_id), smoother_row(2 * y_id + 1)])

    gain = initial_gains.reshape(2, 128)
    hi = lax.reduce_precision(gain, 8, 7)
    mid = lax.reduce_precision(gain - hi, 8, 7)
    weight = jnp.tile(jnp.repeat(1.0 - flags.astype(F32), 2), 2)
    extra = jnp.stack([hi, mid, gain - hi - mid, jnp.broadcast_to(weight, (2, 128))], axis=1)
    extra = jnp.concatenate([extra, jnp.zeros((2, 12, 128), F32)], axis=1).astype(BF16)
    sky = jnp.concatenate([sources.reshape(2, 128, 128), extra], axis=1)
    sky_all = [sky] + over_y(sky)

    half = jax.ShapeDtypeStruct((8, 128, 128), BF16)
    keep, send = call(turn_kernel, (half, half), 1, place, voltages.reshape(8, 128, 256))
    recv = over_core(send)
    packed = call(
        pack_kernel, jax.ShapeDtypeStruct((8, 400, 128), BF16), 1, place, keep, recv, *sky_all
    )
    big = lax.all_to_all(packed, "row", split_axis=0, concat_axis=0, tiled=True)
    other = over_core(big[:, 256:400])
    nat, y_re, y_im, misc = call(
        lay_kernel,
        (
            jax.ShapeDtypeStruct((1024, 256), BF16),
            jax.ShapeDtypeStruct((144, 1024), BF16),
            jax.ShapeDtypeStruct((144, 1024), BF16),
            jax.ShapeDtypeStruct((8, 1024), F32),
        ),
        1,
        place,
        big,
        other,
    )
    static = (nat, y_re, y_im)
    gain_and_m = (jax.ShapeDtypeStruct((8, 1024), F32), jax.ShapeDtypeStruct((144, 256), F32))
    for sweep in range(ITERS):
        if sweep == 0:
            gains, m = call(first_kernel, gain_and_m, 0, misc, *static)
        else:
            near = over_z(update)
            pieces = [update] + near + [over_core(value) for value in near]
            gains, m = call(
                functools.partial(next_kernel, sweep - 1),
                gain_and_m,
                1,
                coef,
                *pieces,
                gains,
                misc,
                *static,
            )
        sums = call(
            collect_kernel, jax.ShapeDtypeStruct((4, 1024), F32), 0, m, *over_x(m), gains, misc, *static
        )
        sums = sums + over_core(sums)
        sums = [sums] + over_y(sums)
        if sweep + 1 < ITERS:
            update = call(
                update_kernel, jax.ShapeDtypeStruct((2, 1024), F32), 0, *sums, gains, misc
            )
    last = call(
        last_update_kernel, jax.ShapeDtypeStruct((8, 40, 128), F32), 0, *sums, gains, misc
    )
    everyone = lax.all_to_all(last, "row", split_axis=0, concat_axis=0, tiled=True)
    out_gains, part = pl.pallas_call(
        finish_kernel,
        out_shape=(
            jax.ShapeDtypeStruct((2, 2, 64), F32),
            jax.ShapeDtypeStruct((8, 128), F32),
        ),
        in_specs=[pl.BlockSpec(memory_space=pltpu.SMEM)] * 2
        + [pl.BlockSpec(memory_space=pltpu.VMEM)] * 2,
        out_specs=(pl.BlockSpec(memory_space=pltpu.VMEM), pl.BlockSpec(memory_space=pltpu.VMEM)),
        scratch_shapes=[pltpu.VMEM((16, 128), F32)],
    )(place, final_coef, everyone, misc)
    whole = sum(over_x(part), part)[0:2, 0 : 2 * ITERS].reshape(2, ITERS, 2)
    return out_gains, whole[:, :, 0] / (whole[:, :, 1] + 1e-06)


def solution(mesh):
    placed = (
        P(None, None, ("row", "col"), "chan"),
        P("chan", None, ("row", "col"), None),
        P("chan", None, ("row", "col")),
        P(("row", "col")),
        P(),
    )
    return jax.shard_map(
        shards,
        mesh=mesh,
        in_specs=placed,
        out_specs=(P("chan", None, ("row", "col")), P("chan", None)),
        check_vma=False,
    )
```

```python
import functools

import jax
import jax.numpy as jnp
from jax import lax
from jax.experimental import pallas as pl
from jax.experimental.pallas import tpu as pltpu
from jax.sharding import PartitionSpec as P


ITERS = 4
F32 = jnp.float32
BF16 = jnp.bfloat16
NT = (((1,), (1,)), ((), ()))


def call(kernel, out_shape, smem_count, *operands, scratch=()):
    in_specs = [pl.BlockSpec(memory_space=pltpu.SMEM)] * smem_count + [
        pl.BlockSpec(memory_space=pltpu.VMEM)
    ] * (len(operands) - smem_count)
    return pl.pallas_call(
        kernel,
        out_shape=out_shape,
        in_specs=in_specs,
        out_specs=jax.tree.map(lambda _: pl.BlockSpec(memory_space=pltpu.VMEM), out_shape),
        scratch_shapes=scratch,
        compiler_params=pltpu.CompilerParams(vmem_limit_bytes=24 * 1024 * 1024),
    )(*operands)


def lanes_merge(first, second):
    lane = lax.broadcasted_iota(jnp.int32, first.shape, first.ndim - 1)
    left = lane < 64
    low = jnp.where(left, first, pltpu.roll(second, 64, first.ndim - 1))
    high = jnp.where(left, pltpu.roll(first, 64, first.ndim - 1), second)
    return low, high


def turn_kernel(place_ref, volt_ref, keep_ref, send_ref):
    core = place_ref[0]
    for chan in range(volt_ref.shape[0]):
        for ref, half in ((keep_ref, core), (send_ref, 1 - core)):
            block = volt_ref[chan, :, pl.ds(pl.multiple_of(half * 128, 128), 128)]
            ref[chan] = block.T


def hop(place_ref, distance):
    return (place_ref[3] + (1 - 2 * place_ref[0]) * distance + 8) & 7


def pack_kernel(place_ref, keep_ref, recv_ref, *out_refs):
    flip = jnp.full((128, 128), place_ref[0], jnp.int32) == 1
    for distance, ref in enumerate(out_refs):
        chan = hop(place_ref, distance)
        own = keep_ref[chan].astype(F32)
        other = recv_ref[chan].astype(F32)
        low, high = lanes_merge(jnp.where(flip, other, own), jnp.where(flip, own, other))
        ref[0:128, :] = low.astype(BF16)
        ref[128:256, :] = high.astype(BF16)


def lay_kernel(place_ref, *refs):
    x_refs = refs[0:8]
    sky_ref, other_ref, nat_ref, yr_ref, yi_ref, misc_ref, gain_ref, m_ref = refs[8:]
    core, block = place_ref[0], place_ref[2]
    for distance, ref in enumerate(x_refs):
        lanes = pl.ds(pl.multiple_of(hop(place_ref, -distance) * 128, 128), 128)
        x_re, x_im = ref[0:128, :], ref[128:256, :]
        yr_ref[0:128, lanes] = x_re
        yi_ref[0:128, lanes] = x_im
        x_re, x_im = x_re.astype(F32), x_im.astype(F32)
        misc_ref[4:5, lanes] = jnp.sum(x_re * x_re + x_im * x_im, axis=0, keepdims=True)
    flip = jnp.full((1, 128), core, jnp.int32) == 1
    for step in range(8):
        z = (2 * place_ref[1] + (place_ref[3] & 1) + step) & 7
        mine = pl.ds(pl.multiple_of(z * 128 + core * 64, 64), 64)
        theirs = pl.ds(pl.multiple_of(z * 128 + (1 - core) * 64, 64), 64)
        nat_ref[mine, 0:128] = sky_ref[step, 0:64, :]
        nat_ref[mine, 128:256] = sky_ref[step, 64:128, :]
        nat_ref[theirs, 0:128] = other_ref[step, 0:64, :]
        nat_ref[theirs, 128:256] = other_ref[step, 64:128, :]
        lanes = pl.ds(pl.multiple_of(z * 128, 128), 128)
        own = sky_ref[step, 128:144, :].astype(F32)
        other = other_ref[step, 128:144, :].astype(F32)
        own_gain = own[0:1] + own[1:2] + own[2:3]
        other_gain = other[0:1] + other[1:2] + other[2:3]
        gain_re, gain_im = lanes_merge(
            jnp.where(flip, other_gain, own_gain), jnp.where(flip, own_gain, other_gain)
        )
        weight, _ = lanes_merge(
            jnp.where(flip, other[3:4], own[3:4]), jnp.where(flip, own[3:4], other[3:4])
        )
        misc_ref[0:1, lanes] = gain_re
        misc_ref[1:2, lanes] = gain_im
        misc_ref[2:3, lanes] = weight
    nat = nat_ref[...]
    row = lax.broadcasted_iota(jnp.int32, (16, 128), 0) + block * 16
    pick = (row == lax.broadcasted_iota(jnp.int32, (16, 128), 1)).astype(BF16)
    yr_ref[128:144, :] = lax.dot_general(
        pick, nat[:, 0:128], NT, preferred_element_type=F32
    ).astype(BF16)
    yi_ref[128:144, :] = lax.dot_general(
        pick, nat[:, 128:256], NT, preferred_element_type=F32
    ).astype(BF16)
    wide = nat.astype(F32)
    square = wide * wide
    hi = square.astype(BF16)
    lo = (square - hi.astype(F32)).astype(BF16)
    ones = jnp.ones((16, 256), BF16)
    alpha = lax.dot_general(ones, hi, NT, preferred_element_type=F32) + lax.dot_general(
        ones, lo, NT, preferred_element_type=F32
    )
    misc_ref[3:4, :] = alpha[0:1]
    misc_ref[5:8, :] = jnp.zeros((3, misc_ref.shape[1]), F32)
    gain_re, gain_im, weight = misc_ref[0:1], misc_ref[1:2], misc_ref[2:3]
    gain_ref[0:1] = gain_re
    gain_ref[1:2] = gain_im
    gain_ref[2:8] = jnp.zeros((6, gain_re.shape[1]), F32)
    spread(gain_re, gain_im, weight, nat_ref, yr_ref, yi_ref, m_ref)


def split(value):
    hi = value.astype(BF16)
    return hi, (value - hi.astype(F32)).astype(BF16)


def spread(gain_re, gain_im, weight, nat_ref, yr_ref, yi_ref, m_ref):
    w_re = weight * gain_re
    w_im = weight * gain_im
    w_pow = weight * (gain_re * gain_re + gain_im * gain_im)
    total = None
    for start in range(0, nat_ref.shape[0], 256):
        lanes = slice(start, start + 256)
        row = lax.broadcasted_iota(jnp.int32, (144, 256), 0) < 128
        c_re = jnp.where(row, w_re[:, lanes], w_pow[:, lanes])
        c_im = jnp.where(row, w_im[:, lanes], 0.0)
        y_re = yr_ref[:, lanes].astype(F32)
        y_im = yi_ref[:, lanes].astype(F32)
        re_hi, re_lo = split(y_re * c_re + y_im * c_im)
        im_hi, im_lo = split(y_re * c_im - y_im * c_re)
        left = jnp.concatenate([re_hi, re_lo, im_hi, im_lo], axis=0)
        part = jnp.dot(left, nat_ref[lanes, :], preferred_element_type=F32)
        total = part if total is None else total + part
    re = total[0:144] + total[144:288]
    im = total[288:432] + total[432:576]
    m_ref[:, 0:128] = re[:, 0:128] - im[:, 128:256]
    m_ref[:, 128:256] = re[:, 128:256] + im[:, 0:128]


def weight_of(near_ref, chan, other):
    value = jnp.where(chan == other, 0.5, 0.0)
    value = value + jnp.where(near_ref[chan, 0] == other, 0.25, 0.0)
    return value + jnp.where(near_ref[chan, 1] == other, 0.25, 0.0)


def next_kernel(
    sweep, place_ref, near_ref, u0, u1, u2, u3, u4, u5, u6, old_ref, misc_ref, nat_ref, yr_ref, yi_ref, gain_ref, m_ref
):
    chan = place_ref[3]
    smooth = weight_of(near_ref, chan, chan) * u0[...]
    for distance, ref in ((-1, u1), (-2, u2), (-3, u3), (1, u4), (2, u5), (3, u6)):
        smooth = smooth + weight_of(near_ref, chan, hop(place_ref, distance)) * ref[...]
    gain_re, gain_im, weight = smooth[0:1], smooth[1:2], misc_ref[2:3]
    diff_re, diff_im = gain_re - old_ref[0:1], gain_im - old_ref[1:2]
    delta = jnp.sum(weight * (diff_re * diff_re + diff_im * diff_im), axis=1, keepdims=True)
    level = jnp.sum(weight * (gain_re * gain_re + gain_im * gain_im), axis=1, keepdims=True)
    lane = lax.broadcasted_iota(jnp.int32, gain_re.shape, 1)
    gain_ref[0:1] = gain_re
    gain_ref[1:2] = gain_im
    gain_ref[2:3] = jnp.where(lane == sweep, delta, old_ref[2:3])
    gain_ref[3:4] = jnp.where(lane == sweep, level, old_ref[3:4])
    gain_ref[4:8] = jnp.zeros((4, gain_re.shape[1]), F32)
    spread(gain_re, gain_im, weight, nat_ref, yr_ref, yi_ref, m_ref)


def collect_kernel(m0, m1, m2, m3, gain_ref, misc_ref, nat_ref, yr_ref, yi_ref, out_ref):
    total = (m0[...] + m1[...]) + (m2[...] + m3[...])
    re, im = total[:, 0:128], total[:, 128:256]
    a_hi, a_lo = split(total)
    b_hi, b_lo = split(jnp.concatenate([im, -re], axis=1))
    left = jnp.concatenate([a_hi, a_lo, b_hi, b_lo], axis=0)
    for start in range(0, nat_ref.shape[0], 256):
        lanes = slice(start, start + 256)
        part = lax.dot_general(left, nat_ref[lanes, :], NT, preferred_element_type=F32)
        z_re = part[0:144] + part[144:288]
        z_im = part[288:432] + part[432:576]
        y_re = yr_ref[:, lanes].astype(F32)
        y_im = yi_ref[:, lanes].astype(F32)
        real = y_re * z_re - y_im * z_im
        imag = y_re * z_im + y_im * z_re
        num_re = jnp.sum(real[0:128], axis=0, keepdims=True)
        num_im = jnp.sum(imag[0:128], axis=0, keepdims=True)
        den = jnp.sum(real[128:144], axis=0, keepdims=True)
        g_re, g_im = gain_ref[0:1, lanes], gain_ref[1:2, lanes]
        weight, alpha, power = (misc_ref[r : r + 1, lanes] for r in (2, 3, 4))
        own = alpha * power * weight
        out_ref[0:1, lanes] = num_re - own * g_re
        out_ref[1:2, lanes] = num_im - own * g_im
        out_ref[2:3, lanes] = den - 0.125 * alpha * alpha * weight * (g_re * g_re + g_im * g_im)
        out_ref[3:4, lanes] = jnp.zeros_like(den)


def updated(n0, n1, n2, n3, gain_ref, misc_ref):
    total = (n0[...] + n1[...]) + (n2[...] + n3[...])
    g_re, g_im = gain_ref[0:1], gain_ref[1:2]
    live = misc_ref[2:3] > 0.5
    den = total[2:3]
    u_re = jnp.where(live, 0.5 * (0.125 * total[0:1] / den + g_re), g_re)
    u_im = jnp.where(live, 0.5 * (0.125 * total[1:2] / den + g_im), g_im)
    return u_re, u_im


def update_kernel(n0, n1, n2, n3, gain_ref, misc_ref, out_ref):
    u_re, u_im = updated(n0, n1, n2, n3, gain_ref, misc_ref)
    out_ref[0:1] = u_re
    out_ref[1:2] = u_im


def last_update_kernel(n0, n1, n2, n3, gain_ref, misc_ref, out_ref):
    u_re, u_im = updated(n0, n1, n2, n3, gain_ref, misc_ref)
    for index, value in enumerate((u_re, u_im, gain_ref[0:1], gain_ref[1:2])):
        for z in range(8):
            row = index * 8 + z
            out_ref[row : row + 1, :] = value[:, z * 128 : z * 128 + 128]
    out_ref[32:34, :] = gain_ref[2:4, 0:128]
    out_ref[34:40, :] = jnp.zeros((6, 128), F32)


def finish_kernel(place_ref, near_ref, *refs):
    pieces = refs[0:8]
    misc_ref, gains_ref, sums_ref, all_ref, scratch = refs[8:]
    core, y_id, z_id = place_ref[0], place_ref[1], place_ref[3]
    for distance, ref in zip((0, -1, -2, -3, -4, 1, 2, 3), pieces):
        all_ref[hop(place_ref, distance)] = ref[...]
    weight = jnp.concatenate([misc_ref[2:3, z * 128 : z * 128 + 128] for z in range(8)], axis=0)
    lane = lax.broadcasted_iota(jnp.int32, (1, 128), 1)
    flip = jnp.full((1, 128), core, jnp.int32) == 1
    sums_ref[...] = jnp.zeros_like(sums_ref)
    for b in range(2):
        chan = 2 * y_id + b
        smooth = weight_of(near_ref, chan, 0) * all_ref[0, 0:16, :]
        for other in range(1, 8):
            smooth = smooth + weight_of(near_ref, chan, other) * all_ref[other, 0:16, :]
        diff = smooth - all_ref[chan, 16:32, :]
        delta = weight * (diff[0:8] * diff[0:8] + diff[8:16] * diff[8:16])
        level = weight * (smooth[0:8] * smooth[0:8] + smooth[8:16] * smooth[8:16])
        delta = jnp.sum(jnp.sum(delta, axis=0, keepdims=True), axis=1, keepdims=True)
        level = jnp.sum(jnp.sum(level, axis=0, keepdims=True), axis=1, keepdims=True)
        newest = lane == ITERS - 1
        sums_ref[b : b + 1, :] = jnp.where(newest, delta, all_ref[chan, 32:33, :])
        sums_ref[2 + b : 3 + b, :] = jnp.where(newest, level, all_ref[chan, 33:34, :])
        scratch[...] = smooth
        for part in range(2):
            row = scratch[pl.ds(part * 8 + z_id, 1), :]
            row = jnp.where(flip, pltpu.roll(row, 64, 1), row)
            gains_ref[b, part : part + 1, :] = row[:, 0:64]


def ratio_kernel(p0, p1, p2, p3, out_ref):
    total = (p0[...] + p1[...]) + (p2[...] + p3[...])
    out_ref[...] = total[0:2, 0:ITERS] / (total[2:4, 0:ITERS] + 1e-06)


def shards(voltages, sources, initial_gains, flags, neighbours):
    y_id, z_id, col_id = lax.axis_index("chan"), lax.axis_index("row"), lax.axis_index("col")
    core = col_id % 2
    place = jnp.stack([core, y_id, y_id * 2 + core, z_id]).astype(jnp.int32)

    def over_core(value):
        return lax.ppermute(value, "col", [(i, i ^ 1) for i in range(8)])

    def over_x(value):
        return [
            lax.ppermute(value, "col", [(i, (i + 2 * d) % 8) for i in range(8)]) for d in (1, 2, 3)
        ]

    def over_y(value):
        return [lax.ppermute(value, "chan", [(i, (i + d) % 4) for i in range(4)]) for d in (1, 2, 3)]

    def over_z(value, distance):
        pairs = [
            (z * 8 + c, (z + (1 - 2 * (c % 2)) * distance) % 8 * 8 + c)
            for z in range(8)
            for c in range(8)
        ]
        return lax.ppermute(value, ("row", "col"), pairs)

    def sky_to_channel(value, step):
        pairs = []
        for y in range(4):
            for z in range(8):
                target = (z - step) % 8
                pairs.append((y * 8 + z, target // 2 * 8 + 2 * y + target % 2))
        return lax.ppermute(value, ("chan", "row"), pairs)

    gain = initial_gains.reshape(2, 128)
    hi = lax.reduce_precision(gain, 8, 7)
    mid = lax.reduce_precision(gain - hi, 8, 7)
    weight = jnp.tile(jnp.repeat(1.0 - flags.astype(F32), 2), 2)
    extra = jnp.stack([hi, mid, gain - hi - mid, jnp.broadcast_to(weight, (2, 128))], axis=1)
    extra = jnp.concatenate([extra, jnp.zeros((2, 12, 128), F32)], axis=1).astype(BF16)
    sky = jnp.concatenate([sources.reshape(2, 128, 128), extra], axis=1)
    odd = z_id % 2
    by_step = [lax.dynamic_index_in_dim(sky, (odd + b) % 2, 0, keepdims=False) for b in range(2)]
    sky = jnp.stack([sky_to_channel(by_step[step % 2], step) for step in range(8)])

    half = jax.ShapeDtypeStruct((8, 128, 128), BF16)
    keep, send = call(turn_kernel, (half, half), 1, place, voltages.reshape(8, 128, 256))
    packed = call(
        pack_kernel,
        (jax.ShapeDtypeStruct((256, 128), BF16),) * 8,
        1,
        place,
        keep,
        over_core(send),
    )
    volts = [packed[0]] + [over_z(packed[d], d) for d in range(1, 8)]
    nat, y_re, y_im, misc, gains, m = call(
        lay_kernel,
        (
            jax.ShapeDtypeStruct((1024, 256), BF16),
            jax.ShapeDtypeStruct((144, 1024), BF16),
            jax.ShapeDtypeStruct((144, 1024), BF16),
            jax.ShapeDtypeStruct((8, 1024), F32),
            jax.ShapeDtypeStruct((8, 1024), F32),
            jax.ShapeDtypeStruct((144, 256), F32),
        ),
        1,
        place,
        *volts,
        sky,
        over_core(sky),
    )
    static = (nat, y_re, y_im)
    for sweep in range(ITERS):
        sums = call(
            collect_kernel, jax.ShapeDtypeStruct((4, 1024), F32), 0, m, *over_x(m), gains, misc, *static
        )
        sums = sums + over_core(sums)
        sums = [sums] + over_y(sums)
        if sweep + 1 == ITERS:
            break
        update = call(
            update_kernel, jax.ShapeDtypeStruct((2, 1024), F32), 0, *sums, gains, misc
        )
        near = [over_z(update, d) for d in (1, 2, 3)]
        gains, m = call(
            functools.partial(next_kernel, sweep),
            (jax.ShapeDtypeStruct((8, 1024), F32), jax.ShapeDtypeStruct((144, 256), F32)),
            2,
            place,
            neighbours,
            update,
            *near,
            *[over_core(value) for value in near],
            gains,
            misc,
            *static,
        )
    last = call(last_update_kernel, jax.ShapeDtypeStruct((40, 128), F32), 0, *sums, gains, misc)
    near = [over_z(last, d) for d in (1, 2, 3, 4)]
    out_gains, part = call(
        finish_kernel,
        (jax.ShapeDtypeStruct((2, 2, 64), F32), jax.ShapeDtypeStruct((8, 128), F32)),
        2,
        place,
        neighbours,
        last,
        *near,
        *[over_core(value) for value in near[0:3]],
        misc,
        scratch=[pltpu.VMEM((8, 40, 128), F32), pltpu.VMEM((16, 128), F32)],
    )
    step_change = call(
        ratio_kernel, jax.ShapeDtypeStruct((2, ITERS), F32), 0, part, *over_x(part)
    )
    return out_gains, step_change


def solution(mesh):
    placed = (
        P(None, None, ("row", "col"), "chan"),
        P("chan", None, ("row", "col"), None),
        P("chan", None, ("row", "col")),
        P(("row", "col")),
        P(),
    )
    return jax.shard_map(
        shards,
        mesh=mesh,
        in_specs=placed,
        out_specs=(P("chan", None, ("row", "col")), P("chan", None)),
        check_vma=False,
    )
```

```python
import functools

import jax
import jax.numpy as jnp
from jax import lax
from jax.experimental import pallas as pl
from jax.experimental.pallas import tpu as pltpu
from jax.sharding import PartitionSpec as P


ITERS = 4
F32 = jnp.float32
BF16 = jnp.bfloat16
NT = (((1,), (1,)), ((), ()))


def call(kernel, out_shape, smem_count, *operands, scratch=()):
    in_specs = [pl.BlockSpec(memory_space=pltpu.SMEM)] * smem_count + [
        pl.BlockSpec(memory_space=pltpu.VMEM)
    ] * (len(operands) - smem_count)
    return pl.pallas_call(
        kernel,
        out_shape=out_shape,
        in_specs=in_specs,
        out_specs=jax.tree.map(lambda _: pl.BlockSpec(memory_space=pltpu.VMEM), out_shape),
        scratch_shapes=scratch,
        compiler_params=pltpu.CompilerParams(vmem_limit_bytes=24 * 1024 * 1024),
    )(*operands)


def lanes_merge(first, second):
    lane = lax.broadcasted_iota(jnp.int32, first.shape, first.ndim - 1)
    left = lane < 64
    low = jnp.where(left, first, pltpu.roll(second, 64, first.ndim - 1))
    high = jnp.where(left, pltpu.roll(first, 64, first.ndim - 1), second)
    return low, high


def turn_kernel(place_ref, volt_ref, keep_ref, send_ref):
    core = place_ref[0]
    for chan in range(volt_ref.shape[0]):
        for ref, half in ((keep_ref, core), (send_ref, 1 - core)):
            block = volt_ref[chan, :, pl.ds(pl.multiple_of(half * 128, 128), 128)]
            ref[chan] = block.T


def hop(place_ref, distance):
    return (place_ref[3] + (1 - 2 * place_ref[0]) * distance + 8) & 7


def pack_kernel(place_ref, keep_ref, recv_ref, s0, s1, s2, s3, out_ref):
    core, y_id = place_ref[0], place_ref[1]
    flip = jnp.full((128, 128), core, jnp.int32) == 1
    for chan in range(keep_ref.shape[0]):
        own = keep_ref[chan].astype(F32)
        other = recv_ref[chan].astype(F32)
        low, high = lanes_merge(jnp.where(flip, other, own), jnp.where(flip, own, other))
        out_ref[chan, 0:128, :] = low.astype(BF16)
        out_ref[chan, 128:256, :] = high.astype(BF16)
    for step, ref in enumerate((s0, s1, s2, s3)):
        owner = lax.rem(y_id + 4 - step, 4)
        for b in range(2):
            out_ref[2 * owner + b, 256:400, :] = ref[b]


def lay_kernel(
    place_ref, big_ref, other_ref, nat_ref, yr_ref, yi_ref, misc_ref, gain_ref, m_ref, code_ref
):
    core, block = place_ref[0], place_ref[2]
    flip = jnp.full((1, 128), core, jnp.int32) == 1
    for z in range(8):
        mine = pl.ds(pl.multiple_of(z * 128 + core * 64, 64), 64)
        theirs = pl.ds(pl.multiple_of(z * 128 + (1 - core) * 64, 64), 64)
        nat_ref[mine, 0:128] = big_ref[z, 256:320, :]
        nat_ref[mine, 128:256] = big_ref[z, 320:384, :]
        nat_ref[theirs, 0:128] = other_ref[z, 0:64, :]
        nat_ref[theirs, 128:256] = other_ref[z, 64:128, :]
        lanes = slice(z * 128, z * 128 + 128)
        x_re, x_im = big_ref[z, 0:128, :], big_ref[z, 128:256, :]
        yr_ref[0:128, lanes] = x_re
        yi_ref[0:128, lanes] = x_im
        x_re, x_im = x_re.astype(F32), x_im.astype(F32)
        own = big_ref[z, 384:400, :].astype(F32)
        other = other_ref[z, 128:144, :].astype(F32)
        own_gain = own[0:1] + own[1:2] + own[2:3]
        other_gain = other[0:1] + other[1:2] + other[2:3]
        gain_re, gain_im = lanes_merge(
            jnp.where(flip, other_gain, own_gain), jnp.where(flip, own_gain, other_gain)
        )
        weight, _ = lanes_merge(
            jnp.where(flip, other[3:4], own[3:4]), jnp.where(flip, own[3:4], other[3:4])
        )
        misc_ref[0:1, lanes] = gain_re
        misc_ref[1:2, lanes] = gain_im
        misc_ref[2:3, lanes] = weight
        misc_ref[4:5, lanes] = jnp.sum(x_re * x_re + x_im * x_im, axis=0, keepdims=True)
    nat = nat_ref[...]
    row = lax.broadcasted_iota(jnp.int32, (16, 128), 0) + block * 16
    pick = (row == lax.broadcasted_iota(jnp.int32, (16, 128), 1)).astype(BF16)
    yr_ref[128:144, :] = lax.dot_general(
        pick, nat[:, 0:128], NT, preferred_element_type=F32
    ).astype(BF16)
    yi_ref[128:144, :] = lax.dot_general(
        pick, nat[:, 128:256], NT, preferred_element_type=F32
    ).astype(BF16)
    wide = nat.astype(F32)
    square = wide * wide
    hi = square.astype(BF16)
    lo = (square - hi.astype(F32)).astype(BF16)
    ones = jnp.ones((16, 256), BF16)
    alpha = lax.dot_general(ones, hi, NT, preferred_element_type=F32) + lax.dot_general(
        ones, lo, NT, preferred_element_type=F32
    )
    misc_ref[3:4, :] = alpha[0:1]
    misc_ref[5:8, :] = jnp.zeros((3, misc_ref.shape[1]), F32)
    gain_re, gain_im, weight = misc_ref[0:1], misc_ref[1:2], misc_ref[2:3]
    gain_ref[0:1] = gain_re
    gain_ref[1:2] = gain_im
    gain_ref[2:8] = jnp.zeros((6, gain_re.shape[1]), F32)
    spread(gain_re, gain_im, weight, nat_ref, yr_ref, yi_ref, m_ref, code_ref)


def split(value):
    hi = value.astype(BF16)
    return hi, (value - hi.astype(F32)).astype(BF16)


SPAN = 83.0
BLOCKS = ((0, 128), (128, 144))


def encode(m_ref, code_ref):
    scales = []
    for start, end in BLOCKS:
        value = m_ref[start:end, :]
        size = jnp.abs(value)
        scale = jnp.maximum(jnp.max(size, axis=0, keepdims=True) * 1.01, 1e-30)
        scale = scale.astype(BF16).astype(F32)
        code = jnp.exp(size * (SPAN / scale))
        code_ref[start:end, :] = jnp.where(value < 0, -code, code).astype(BF16)
        scales.append(scale)
    scales.append(jnp.zeros((14, 256), F32))
    code_ref[144:160, :] = jnp.concatenate(scales, axis=0).astype(BF16)


def decode(code_ref):
    scales = code_ref[144:160, :].astype(F32)
    parts = []
    for index, (start, end) in enumerate(BLOCKS):
        code = code_ref[start:end, :].astype(F32)
        size = jnp.log(jnp.abs(code)) * (scales[index : index + 1] * (1 / SPAN))
        parts.append(jnp.where(code < 0, -size, size))
    return jnp.concatenate(parts, axis=0)


def spread(gain_re, gain_im, weight, nat_ref, yr_ref, yi_ref, m_ref, code_ref):
    w_re = weight * gain_re
    w_im = weight * gain_im
    w_pow = weight * (gain_re * gain_re + gain_im * gain_im)
    total = None
    for start in range(0, nat_ref.shape[0], 256):
        lanes = slice(start, start + 256)
        row = lax.broadcasted_iota(jnp.int32, (144, 256), 0) < 128
        c_re = jnp.where(row, w_re[:, lanes], w_pow[:, lanes])
        c_im = jnp.where(row, w_im[:, lanes], 0.0)
        y_re = yr_ref[:, lanes].astype(F32)
        y_im = yi_ref[:, lanes].astype(F32)
        re_hi, re_lo = split(y_re * c_re + y_im * c_im)
        im_hi, im_lo = split(y_re * c_im - y_im * c_re)
        left = jnp.concatenate([re_hi, re_lo, im_hi, im_lo], axis=0)
        part = jnp.dot(left, nat_ref[lanes, :], preferred_element_type=F32)
        total = part if total is None else total + part
    re = total[0:144] + total[144:288]
    im = total[288:432] + total[432:576]
    m_ref[:, 0:128] = re[:, 0:128] - im[:, 128:256]
    m_ref[:, 128:256] = re[:, 128:256] + im[:, 0:128]
    encode(m_ref, code_ref)


def weight_of(near_ref, chan, other):
    value = jnp.where(chan == other, 0.5, 0.0)
    value = value + jnp.where(near_ref[chan, 0] == other, 0.25, 0.0)
    return value + jnp.where(near_ref[chan, 1] == other, 0.25, 0.0)


def next_kernel(
    sweep, place_ref, near_ref, u0, u1, u2, u3, u4, u5, u6, old_ref, misc_ref, nat_ref, yr_ref, yi_ref, gain_ref, m_ref, code_ref
):
    chan = place_ref[3]
    smooth = weight_of(near_ref, chan, chan) * u0[...]
    for distance, ref in ((-1, u1), (-2, u2), (-3, u3), (1, u4), (2, u5), (3, u6)):
        smooth = smooth + weight_of(near_ref, chan, hop(place_ref, distance)) * ref[...]
    gain_re, gain_im, weight = smooth[0:1], smooth[1:2], misc_ref[2:3]
    diff_re, diff_im = gain_re - old_ref[0:1], gain_im - old_ref[1:2]
    delta = jnp.sum(weight * (diff_re * diff_re + diff_im * diff_im), axis=1, keepdims=True)
    level = jnp.sum(weight * (gain_re * gain_re + gain_im * gain_im), axis=1, keepdims=True)
    lane = lax.broadcasted_iota(jnp.int32, gain_re.shape, 1)
    gain_ref[0:1] = gain_re
    gain_ref[1:2] = gain_im
    gain_ref[2:3] = jnp.where(lane == sweep, delta, old_ref[2:3])
    gain_ref[3:4] = jnp.where(lane == sweep, level, old_ref[3:4])
    gain_ref[4:8] = jnp.zeros((4, gain_re.shape[1]), F32)
    spread(gain_re, gain_im, weight, nat_ref, yr_ref, yi_ref, m_ref, code_ref)


def collect_kernel(m0, m1, m2, m3, gain_ref, misc_ref, nat_ref, yr_ref, yi_ref, out_ref):
    total = (m0[...] + decode(m1)) + (decode(m2) + decode(m3))
    re, im = total[:, 0:128], total[:, 128:256]
    a_hi, a_lo = split(total)
    b_hi, b_lo = split(jnp.concatenate([im, -re], axis=1))
    left = jnp.concatenate([a_hi, a_lo, b_hi, b_lo], axis=0)
    for start in range(0, nat_ref.shape[0], 256):
        lanes = slice(start, start + 256)
        part = lax.dot_general(left, nat_ref[lanes, :], NT, preferred_element_type=F32)
        z_re = part[0:144] + part[144:288]
        z_im = part[288:432] + part[432:576]
        y_re = yr_ref[:, lanes].astype(F32)
        y_im = yi_ref[:, lanes].astype(F32)
        real = y_re * z_re - y_im * z_im
        imag = y_re * z_im + y_im * z_re
        num_re = jnp.sum(real[0:128], axis=0, keepdims=True)
        num_im = jnp.sum(imag[0:128], axis=0, keepdims=True)
        den = jnp.sum(real[128:144], axis=0, keepdims=True)
        g_re, g_im = gain_ref[0:1, lanes], gain_ref[1:2, lanes]
        weight, alpha, power = (misc_ref[r : r + 1, lanes] for r in (2, 3, 4))
        own = alpha * power * weight
        out_ref[0:1, lanes] = num_re - own * g_re
        out_ref[1:2, lanes] = num_im - own * g_im
        out_ref[2:3, lanes] = den - 0.125 * alpha * alpha * weight * (g_re * g_re + g_im * g_im)
        out_ref[3:4, lanes] = jnp.zeros_like(den)


def updated(n0, n1, n2, n3, gain_ref, misc_ref):
    total = (n0[...] + n1[...]) + (n2[...] + n3[...])
    g_re, g_im = gain_ref[0:1], gain_ref[1:2]
    live = misc_ref[2:3] > 0.5
    den = total[2:3]
    u_re = jnp.where(live, 0.5 * (0.125 * total[0:1] / den + g_re), g_re)
    u_im = jnp.where(live, 0.5 * (0.125 * total[1:2] / den + g_im), g_im)
    return u_re, u_im


def update_kernel(n0, n1, n2, n3, gain_ref, misc_ref, out_ref):
    u_re, u_im = updated(n0, n1, n2, n3, gain_ref, misc_ref)
    out_ref[0:1] = u_re
    out_ref[1:2] = u_im


def last_update_kernel(n0, n1, n2, n3, gain_ref, misc_ref, out_ref):
    u_re, u_im = updated(n0, n1, n2, n3, gain_ref, misc_ref)
    for index, value in enumerate((u_re, u_im, gain_ref[0:1], gain_ref[1:2])):
        for z in range(8):
            row = index * 8 + z
            out_ref[row : row + 1, :] = value[:, z * 128 : z * 128 + 128]
    out_ref[32:34, :] = gain_ref[2:4, 0:128]
    out_ref[34:40, :] = jnp.zeros((6, 128), F32)


def finish_kernel(place_ref, near_ref, *refs):
    pieces = refs[0:8]
    misc_ref, gains_ref, sums_ref, all_ref, scratch = refs[8:]
    core, y_id, z_id = place_ref[0], place_ref[1], place_ref[3]
    for distance, ref in zip((0, -1, -2, -3, -4, 1, 2, 3), pieces):
        all_ref[hop(place_ref, distance)] = ref[...]
    weight = jnp.concatenate([misc_ref[2:3, z * 128 : z * 128 + 128] for z in range(8)], axis=0)
    lane = lax.broadcasted_iota(jnp.int32, (1, 128), 1)
    flip = jnp.full((1, 128), core, jnp.int32) == 1
    sums_ref[...] = jnp.zeros_like(sums_ref)
    for b in range(2):
        chan = 2 * y_id + b
        smooth = weight_of(near_ref, chan, 0) * all_ref[0, 0:16, :]
        for other in range(1, 8):
            smooth = smooth + weight_of(near_ref, chan, other) * all_ref[other, 0:16, :]
        diff = smooth - all_ref[chan, 16:32, :]
        delta = weight * (diff[0:8] * diff[0:8] + diff[8:16] * diff[8:16])
        level = weight * (smooth[0:8] * smooth[0:8] + smooth[8:16] * smooth[8:16])
        delta = jnp.sum(jnp.sum(delta, axis=0, keepdims=True), axis=1, keepdims=True)
        level = jnp.sum(jnp.sum(level, axis=0, keepdims=True), axis=1, keepdims=True)
        newest = lane == ITERS - 1
        sums_ref[b : b + 1, :] = jnp.where(newest, delta, all_ref[chan, 32:33, :])
        sums_ref[2 + b : 3 + b, :] = jnp.where(newest, level, all_ref[chan, 33:34, :])
        scratch[...] = smooth
        for part in range(2):
            row = scratch[pl.ds(part * 8 + z_id, 1), :]
            row = jnp.where(flip, pltpu.roll(row, 64, 1), row)
            gains_ref[b, part : part + 1, :] = row[:, 0:64]


def ratio_kernel(p0, p1, p2, p3, out_ref):
    total = (p0[...] + p1[...]) + (p2[...] + p3[...])
    out_ref[...] = total[0:2, 0:ITERS] / (total[2:4, 0:ITERS] + 1e-06)


def shards(voltages, sources, initial_gains, flags, neighbours):
    y_id, z_id, col_id = lax.axis_index("chan"), lax.axis_index("row"), lax.axis_index("col")
    core = col_id % 2
    place = jnp.stack([core, y_id, y_id * 2 + core, z_id]).astype(jnp.int32)

    def over_core(value):
        return lax.ppermute(value, "col", [(i, i ^ 1) for i in range(8)])

    def over_x(value):
        return [
            lax.ppermute(value, "col", [(i, (i + 2 * d) % 8) for i in range(8)]) for d in (1, 2, 3)
        ]

    def over_y(value):
        return [lax.ppermute(value, "chan", [(i, (i + d) % 4) for i in range(4)]) for d in (1, 2, 3)]

    def over_z(value, distance):
        pairs = [
            (z * 8 + c, (z + (1 - 2 * (c % 2)) * distance) % 8 * 8 + c)
            for z in range(8)
            for c in range(8)
        ]
        return lax.ppermute(value, ("row", "col"), pairs)

    gain = initial_gains.reshape(2, 128)
    hi = lax.reduce_precision(gain, 8, 7)
    mid = lax.reduce_precision(gain - hi, 8, 7)
    weight = jnp.tile(jnp.repeat(1.0 - flags.astype(F32), 2), 2)
    extra = jnp.stack([hi, mid, gain - hi - mid, jnp.broadcast_to(weight, (2, 128))], axis=1)
    extra = jnp.concatenate([extra, jnp.zeros((2, 12, 128), F32)], axis=1).astype(BF16)
    sky = jnp.concatenate([sources.reshape(2, 128, 128), extra], axis=1)
    sky_all = [sky] + over_y(sky)

    half = jax.ShapeDtypeStruct((8, 128, 128), BF16)
    keep, send = call(turn_kernel, (half, half), 1, place, voltages.reshape(8, 128, 256))
    recv = over_core(send)
    packed = call(
        pack_kernel, jax.ShapeDtypeStruct((8, 400, 128), BF16), 1, place, keep, recv, *sky_all
    )
    big = lax.all_to_all(packed, "row", split_axis=0, concat_axis=0, tiled=True)
    nat, y_re, y_im, misc, gains, m, code = call(
        lay_kernel,
        (
            jax.ShapeDtypeStruct((1024, 256), BF16),
            jax.ShapeDtypeStruct((144, 1024), BF16),
            jax.ShapeDtypeStruct((144, 1024), BF16),
            jax.ShapeDtypeStruct((8, 1024), F32),
            jax.ShapeDtypeStruct((8, 1024), F32),
            jax.ShapeDtypeStruct((144, 256), F32),
            jax.ShapeDtypeStruct((160, 256), BF16),
        ),
        1,
        place,
        big,
        over_core(big[:, 256:400]),
    )
    static = (nat, y_re, y_im)
    for sweep in range(ITERS):
        sums = call(
            collect_kernel, jax.ShapeDtypeStruct((4, 1024), F32), 0, m, *over_x(code), gains, misc, *static
        )
        sums = sums + over_core(sums)
        sums = [sums] + over_y(sums)
        if sweep + 1 == ITERS:
            break
        update = call(
            update_kernel, jax.ShapeDtypeStruct((2, 1024), F32), 0, *sums, gains, misc
        )
        near = [over_z(update, d) for d in (1, 2, 3)]
        gains, m, code = call(
            functools.partial(next_kernel, sweep),
            (
                jax.ShapeDtypeStruct((8, 1024), F32),
                jax.ShapeDtypeStruct((144, 256), F32),
                jax.ShapeDtypeStruct((160, 256), BF16),
            ),
            2,
            place,
            neighbours,
            update,
            *near,
            *[over_core(value) for value in near],
            gains,
            misc,
            *static,
        )
    last = call(last_update_kernel, jax.ShapeDtypeStruct((40, 128), F32), 0, *sums, gains, misc)
    near = [over_z(last, d) for d in (1, 2, 3, 4)]
    out_gains, part = call(
        finish_kernel,
        (jax.ShapeDtypeStruct((2, 2, 64), F32), jax.ShapeDtypeStruct((8, 128), F32)),
        2,
        place,
        neighbours,
        last,
        *near,
        *[over_core(value) for value in near[0:3]],
        misc,
        scratch=[pltpu.VMEM((8, 40, 128), F32), pltpu.VMEM((16, 128), F32)],
    )
    step_change = call(
        ratio_kernel, jax.ShapeDtypeStruct((2, ITERS), F32), 0, part, *over_x(part)
    )
    return out_gains, step_change


def solution(mesh):
    placed = (
        P(None, None, ("row", "col"), "chan"),
        P("chan", None, ("row", "col"), None),
        P("chan", None, ("row", "col")),
        P(("row", "col")),
        P(),
    )
    return jax.shard_map(
        shards,
        mesh=mesh,
        in_specs=placed,
        out_specs=(P("chan", None, ("row", "col")), P("chan", None)),
        check_vma=False,
    )
```

```python
import functools

import jax
import jax.numpy as jnp
from jax import lax
from jax.experimental import pallas as pl
from jax.experimental.pallas import tpu as pltpu
from jax.sharding import PartitionSpec as P


ITERS = 4
F32 = jnp.float32
BF16 = jnp.bfloat16
NT = (((1,), (1,)), ((), ()))


def call(kernel, out_shape, smem_count, *operands, scratch=()):
    in_specs = [pl.BlockSpec(memory_space=pltpu.SMEM)] * smem_count + [
        pl.BlockSpec(memory_space=pltpu.VMEM)
    ] * (len(operands) - smem_count)
    return pl.pallas_call(
        kernel,
        out_shape=out_shape,
        in_specs=in_specs,
        out_specs=jax.tree.map(lambda _: pl.BlockSpec(memory_space=pltpu.VMEM), out_shape),
        scratch_shapes=scratch,
        compiler_params=pltpu.CompilerParams(vmem_limit_bytes=24 * 1024 * 1024),
    )(*operands)


def lanes_merge(first, second):
    lane = lax.broadcasted_iota(jnp.int32, first.shape, first.ndim - 1)
    left = lane < 64
    low = jnp.where(left, first, pltpu.roll(second, 64, first.ndim - 1))
    high = jnp.where(left, pltpu.roll(first, 64, first.ndim - 1), second)
    return low, high


def turn_kernel(volt_ref, keep_ref, send_ref):
    core = lax.axis_index("col") % 2
    for chan in range(volt_ref.shape[0]):
        for ref, half in ((keep_ref, core), (send_ref, 1 - core)):
            block = volt_ref[chan, :, pl.ds(pl.multiple_of(half * 128, 128), 128)]
            ref[chan] = block.T


def place():
    return lax.axis_index("col") % 2, lax.axis_index("chan"), lax.axis_index("row")


def partner(z, core, distance):
    if distance == 4:
        return (z + 4) % 8
    group = z // 2 if distance == 2 else z
    return (z + distance * (1 - 2 * ((group + core) % 2)) + 8) % 8


def pack_kernel(keep_ref, recv_ref, s0, s1, s2, s3, out_ref):
    core, y_id, _ = place()
    flip = jnp.full((128, 128), core, jnp.int32) == 1
    for chan in range(keep_ref.shape[0]):
        own = keep_ref[chan].astype(F32)
        other = recv_ref[chan].astype(F32)
        low, high = lanes_merge(jnp.where(flip, other, own), jnp.where(flip, own, other))
        out_ref[chan, 0:128, :] = low.astype(BF16)
        out_ref[chan, 128:256, :] = high.astype(BF16)
    for step, ref in enumerate((s0, s1, s2, s3)):
        owner = lax.rem(y_id + 4 - step, 4)
        for b in range(2):
            out_ref[2 * owner + b, 256:400, :] = ref[b]


def lay_kernel(
    big_ref, other_ref, nat_ref, yr_ref, yi_ref, misc_ref, gain_ref, m_ref, code_ref
):
    core, y_id, _ = place()
    block = 2 * y_id + core
    flip = jnp.full((1, 128), core, jnp.int32) == 1
    for z in range(8):
        mine = pl.ds(pl.multiple_of(z * 128 + core * 64, 64), 64)
        theirs = pl.ds(pl.multiple_of(z * 128 + (1 - core) * 64, 64), 64)
        nat_ref[mine, 0:128] = big_ref[z, 256:320, :]
        nat_ref[mine, 128:256] = big_ref[z, 320:384, :]
        nat_ref[theirs, 0:128] = other_ref[z, 0:64, :]
        nat_ref[theirs, 128:256] = other_ref[z, 64:128, :]
        lanes = slice(z * 128, z * 128 + 128)
        x_re, x_im = big_ref[z, 0:128, :], big_ref[z, 128:256, :]
        yr_ref[0:128, lanes] = x_re
        yi_ref[0:128, lanes] = x_im
        own = big_ref[z, 384:400, :].astype(F32)
        other = other_ref[z, 128:144, :].astype(F32)
        own_gain = own[0:1] + own[1:2] + own[2:3]
        other_gain = other[0:1] + other[1:2] + other[2:3]
        gain_re, gain_im = lanes_merge(
            jnp.where(flip, other_gain, own_gain), jnp.where(flip, own_gain, other_gain)
        )
        weight, _ = lanes_merge(
            jnp.where(flip, other[3:4], own[3:4]), jnp.where(flip, own[3:4], other[3:4])
        )
        misc_ref[0:1, lanes] = gain_re
        misc_ref[1:2, lanes] = gain_im
        misc_ref[2:3, lanes] = weight
    nat = nat_ref[...]
    row = lax.broadcasted_iota(jnp.int32, (16, 128), 0) + block * 16
    pick = (row == lax.broadcasted_iota(jnp.int32, (16, 128), 1)).astype(BF16)
    yr_ref[128:144, :] = lax.dot_general(
        pick, nat[:, 0:128], NT, preferred_element_type=F32
    ).astype(BF16)
    yi_ref[128:144, :] = lax.dot_general(
        pick, nat[:, 128:256], NT, preferred_element_type=F32
    ).astype(BF16)
    gain_re, gain_im, weight = misc_ref[0:1], misc_ref[1:2], misc_ref[2:3]
    gain_ref[0:1] = gain_re
    gain_ref[1:2] = gain_im
    spread(gain_re, gain_im, weight, nat_ref, yr_ref, yi_ref, m_ref, code_ref)


def split(value):
    hi = value.astype(BF16)
    return hi, (value - hi.astype(F32)).astype(BF16)


def power_kernel(nat_ref, yr_ref, yi_ref, misc_ref, out_ref, weight_ref):
    wide = nat_ref[...].astype(F32)
    square = wide * wide
    hi = square.astype(BF16)
    lo = (square - hi.astype(F32)).astype(BF16)
    ones = jnp.ones((16, 256), BF16)
    alpha = lax.dot_general(ones, hi, NT, preferred_element_type=F32) + lax.dot_general(
        ones, lo, NT, preferred_element_type=F32
    )
    out_ref[0:1] = alpha[0:1]
    x_re, x_im = yr_ref[0:128].astype(F32), yi_ref[0:128].astype(F32)
    out_ref[1:2] = jnp.sum(x_re * x_re + x_im * x_im, axis=0, keepdims=True)
    for z in range(8):
        weight_ref[z : z + 1, :] = misc_ref[2:3, z * 128 : z * 128 + 128]


SPAN = 83.0
BLOCKS = ((0, 128), (128, 144))


def encode(m_ref, code_ref):
    scales = []
    for start, end in BLOCKS:
        value = m_ref[start:end, :]
        size = jnp.abs(value)
        scale = jnp.maximum(jnp.max(size, axis=0, keepdims=True) * 1.01, 1e-30)
        scale = scale.astype(BF16).astype(F32)
        code = jnp.exp(size * (SPAN / scale))
        code_ref[start:end, :] = jnp.where(value < 0, -code, code).astype(BF16)
        scales.append(scale)
    scales.append(jnp.zeros((14, 256), F32))
    code_ref[144:160, :] = jnp.concatenate(scales, axis=0).astype(BF16)


def decode(code_ref):
    scales = code_ref[144:160, :].astype(F32)
    parts = []
    for index, (start, end) in enumerate(BLOCKS):
        code = code_ref[start:end, :].astype(F32)
        size = jnp.log(jnp.abs(code)) * (scales[index : index + 1] * (1 / SPAN))
        parts.append(jnp.where(code < 0, -size, size))
    return jnp.concatenate(parts, axis=0)


def spread(gain_re, gain_im, weight, nat_ref, yr_ref, yi_ref, m_ref, code_ref):
    w_re = weight * gain_re
    w_im = weight * gain_im
    w_pow = weight * (gain_re * gain_re + gain_im * gain_im)
    total = None
    for start in range(0, nat_ref.shape[0], 256):
        lanes = slice(start, start + 256)
        row = lax.broadcasted_iota(jnp.int32, (144, 256), 0) < 128
        c_re = jnp.where(row, w_re[:, lanes], w_pow[:, lanes])
        c_im = jnp.where(row, w_im[:, lanes], 0.0)
        y_re = yr_ref[:, lanes].astype(F32)
        y_im = yi_ref[:, lanes].astype(F32)
        re_hi, re_lo = split(y_re * c_re + y_im * c_im)
        im_hi, im_lo = split(y_re * c_im - y_im * c_re)
        left = jnp.concatenate([re_hi, re_lo, im_hi, im_lo], axis=0)
        part = jnp.dot(left, nat_ref[lanes, :], preferred_element_type=F32)
        total = part if total is None else total + part
    re = total[0:144] + total[144:288]
    im = total[288:432] + total[432:576]
    m_ref[:, 0:128] = re[:, 0:128] - im[:, 128:256]
    m_ref[:, 128:256] = re[:, 128:256] + im[:, 0:128]
    encode(m_ref, code_ref)


def weight_of(near_ref, chan, other):
    value = jnp.where(chan == other, 0.5, 0.0)
    value = value + jnp.where(near_ref[chan, 0] == other, 0.25, 0.0)
    return value + jnp.where(near_ref[chan, 1] == other, 0.25, 0.0)


def sources_of(z, core):
    return [z] + [partner(z, core, d) for d in (1, 2, 3, 4)] + [partner(z, 1 - core, d) for d in (1, 2, 3)]


def coef_kernel(near_ref, power_ref, coef_ref, final_ref, out_ref):
    out_ref[...] = power_ref[...]
    core, y_id, z_id = place()
    for index, other in enumerate(sources_of(z_id, core)):
        coef_ref[index : index + 1, :] = jnp.full((1, 1024), weight_of(near_ref, z_id, other), F32)
        for b in range(2):
            value = weight_of(near_ref, 2 * y_id + b, other)
            final_ref[b, index : index + 1, :] = jnp.full((1, 128), value, F32)


def next_kernel(coef_ref, u0, u1, u2, u3, v1, v2, v3, misc_ref, nat_ref, yr_ref, yi_ref, gain_ref, m_ref, code_ref):
    smooth = coef_ref[0:1] * u0[...]
    for index, ref in ((1, u1), (2, u2), (3, u3), (5, v1), (6, v2), (7, v3)):
        smooth = smooth + coef_ref[index : index + 1] * ref[...]
    gain_ref[...] = smooth
    spread(smooth[0:1], smooth[1:2], misc_ref[2:3], nat_ref, yr_ref, yi_ref, m_ref, code_ref)


def change_kernel(sweep, new_ref, old_ref, misc_ref, changes_ref, out_ref):
    diff = new_ref[...] - old_ref[...]
    lane = lax.broadcasted_iota(jnp.int32, (1, 128), 1)
    for row, value in ((0, diff), (1, new_ref[...])):
        total = jnp.sum(misc_ref[2:3] * value * value, axis=0, keepdims=True)
        total = jnp.sum(total, axis=1, keepdims=True)
        out_ref[row : row + 1] = jnp.where(lane == sweep, total, changes_ref[row : row + 1])


def collect_kernel(m0, m1, m2, m3, gain_ref, misc_ref, power_ref, nat_ref, yr_ref, yi_ref, out_ref):
    total = (m0[...] + decode(m1)) + (decode(m2) + decode(m3))
    re, im = total[:, 0:128], total[:, 128:256]
    a_hi, a_lo = split(total)
    b_hi, b_lo = split(jnp.concatenate([im, -re], axis=1))
    left = jnp.concatenate([a_hi, a_lo, b_hi, b_lo], axis=0)
    for start in range(0, nat_ref.shape[0], 256):
        lanes = slice(start, start + 256)
        part = lax.dot_general(left, nat_ref[lanes, :], NT, preferred_element_type=F32)
        z_re = part[0:144] + part[144:288]
        z_im = part[288:432] + part[432:576]
        y_re = yr_ref[:, lanes].astype(F32)
        y_im = yi_ref[:, lanes].astype(F32)
        real = y_re * z_re - y_im * z_im
        imag = y_re * z_im + y_im * z_re
        num_re = jnp.sum(real[0:128], axis=0, keepdims=True)
        num_im = jnp.sum(imag[0:128], axis=0, keepdims=True)
        den = jnp.sum(real[128:144], axis=0, keepdims=True)
        g_re, g_im = gain_ref[0:1, lanes], gain_ref[1:2, lanes]
        weight = misc_ref[2:3, lanes]
        alpha, power = power_ref[0:1, lanes], power_ref[1:2, lanes]
        own = alpha * power * weight
        out_ref[0:1, lanes] = num_re - own * g_re
        out_ref[1:2, lanes] = num_im - own * g_im
        out_ref[2:3, lanes] = den - 0.125 * alpha * alpha * weight * (g_re * g_re + g_im * g_im)
        out_ref[3:4, lanes] = jnp.zeros_like(den)


def updated(n0, n1, n2, n3, gain_ref, misc_ref):
    total = (n0[...] + n1[...]) + (n2[...] + n3[...])
    g_re, g_im = gain_ref[0:1], gain_ref[1:2]
    live = misc_ref[2:3] > 0.5
    den = total[2:3]
    u_re = jnp.where(live, 0.5 * (0.125 * total[0:1] / den + g_re), g_re)
    u_im = jnp.where(live, 0.5 * (0.125 * total[1:2] / den + g_im), g_im)
    return u_re, u_im


def update_kernel(n0, n1, n2, n3, gain_ref, misc_ref, out_ref):
    u_re, u_im = updated(n0, n1, n2, n3, gain_ref, misc_ref)
    out_ref[0:1] = u_re
    out_ref[1:2] = u_im


def last_update_kernel(n0, n1, n2, n3, gain_ref, misc_ref, changes_ref, out_ref):
    u_re, u_im = updated(n0, n1, n2, n3, gain_ref, misc_ref)
    for index, value in enumerate((u_re, u_im, gain_ref[0:1], gain_ref[1:2])):
        for z in range(8):
            row = index * 8 + z
            out_ref[row : row + 1, :] = value[:, z * 128 : z * 128 + 128]
    out_ref[32:34, :] = changes_ref[...]
    out_ref[34:40, :] = jnp.zeros((6, 128), F32)


def finish_kernel(coef_ref, weight_ref, *refs):
    pieces, (gains_ref, sums_ref, all_ref, smooth_ref) = refs[0:8], refs[8:]
    core, y_id, z_id = place()
    for other, ref in zip(sources_of(z_id, core), pieces):
        all_ref[other] = ref[16:40, :]
    weight = weight_ref[...]
    lane = lax.broadcasted_iota(jnp.int32, (1, 128), 1)
    flip = jnp.full((1, 128), core, jnp.int32) == 1
    for b in range(2):
        smooth = coef_ref[b, 0:1] * pieces[0][0:16, :]
        for index in range(1, 8):
            smooth = smooth + coef_ref[b, index : index + 1] * pieces[index][0:16, :]
        smooth_ref[...] = smooth
        for part in range(2):
            row = smooth_ref[pl.ds(part * 8 + z_id, 1), :]
            row = jnp.where(flip, pltpu.roll(row, 64, 1), row)
            gains_ref[b, part : part + 1, :] = row[:, 0:64]
        past = all_ref[2 * y_id + b]
        diff = smooth - past[0:16]
        for index, value in enumerate((diff, smooth)):
            total = weight * (value[0:8] * value[0:8] + value[8:16] * value[8:16])
            total = jnp.sum(jnp.sum(total, axis=0, keepdims=True), axis=1, keepdims=True)
            row = 2 * index + b
            sums_ref[row : row + 1, :] = jnp.where(
                lane == ITERS - 1, total, past[16 + index : 17 + index]
            )
    sums_ref[4:8, :] = jnp.zeros((4, 128), F32)


def ratio_kernel(p0, p1, p2, p3, out_ref):
    total = (p0[...] + p1[...]) + (p2[...] + p3[...])
    out_ref[...] = total[0:2, 0:ITERS] / (total[2:4, 0:ITERS] + 1e-06)


def shards(voltages, sources, initial_gains, flags, neighbours):
    def over_core(value):
        return lax.ppermute(value, "col", [(i, i ^ 1) for i in range(8)])

    def over_x(value):
        return [
            lax.ppermute(value, "col", [(i, (i + 2 * d) % 8) for i in range(8)]) for d in (2, 1, 3)
        ]

    def over_y(value):
        return [lax.ppermute(value, "chan", [(i, (i + d) % 4) for i in range(4)]) for d in (1, 2, 3)]

    def over_z(value, distance):
        pairs = [(z * 8 + c, partner(z, c % 2, distance) * 8 + c) for z in range(8) for c in range(8)]
        return lax.ppermute(value, ("row", "col"), pairs)

    gain = initial_gains.reshape(2, 128)
    hi = lax.reduce_precision(gain, 8, 7)
    mid = lax.reduce_precision(gain - hi, 8, 7)
    weight = jnp.tile(jnp.repeat(1.0 - flags.astype(F32), 2), 2)
    extra = jnp.stack([hi, mid, gain - hi - mid, jnp.broadcast_to(weight, (2, 128))], axis=1)
    extra = jnp.concatenate([extra, jnp.zeros((2, 12, 128), F32)], axis=1).astype(BF16)
    sky = jnp.concatenate([sources.reshape(2, 128, 128), extra], axis=1)
    sky_all = [sky] + over_y(sky)

    half = jax.ShapeDtypeStruct((8, 128, 128), BF16)
    keep, send = call(turn_kernel, (half, half), 0, voltages.reshape(8, 128, 256))
    recv = over_core(send)
    packed = call(
        pack_kernel, jax.ShapeDtypeStruct((8, 400, 128), BF16), 0, keep, recv, *sky_all
    )
    big = lax.all_to_all(packed, "row", split_axis=0, concat_axis=0, tiled=True)
    gain_shape = jax.ShapeDtypeStruct((2, 1024), F32)
    m_shape = jax.ShapeDtypeStruct((144, 256), F32)
    code_shape = jax.ShapeDtypeStruct((160, 256), BF16)
    nat, y_re, y_im, misc, gains, m, code = call(
        lay_kernel,
        (
            jax.ShapeDtypeStruct((1024, 256), BF16),
            jax.ShapeDtypeStruct((144, 1024), BF16),
            jax.ShapeDtypeStruct((144, 1024), BF16),
            jax.ShapeDtypeStruct((8, 1024), F32),
            gain_shape,
            m_shape,
            code_shape,
        ),
        0,
        big,
        over_core(big[:, 256:400]),
    )
    static = (nat, y_re, y_im)
    power, weight = call(
        power_kernel, (gain_shape, jax.ShapeDtypeStruct((8, 128), F32)), 0, *static, misc
    )
    coef, final_coef, power = call(
        coef_kernel,
        (jax.ShapeDtypeStruct((8, 1024), F32), jax.ShapeDtypeStruct((2, 8, 128), F32), gain_shape),
        1,
        neighbours,
        power,
    )
    changes = jnp.zeros((2, 128), F32)
    for sweep in range(ITERS):
        sums = call(
            collect_kernel,
            jax.ShapeDtypeStruct((4, 1024), F32),
            0,
            m,
            *over_x(code),
            gains,
            misc,
            power,
            *static,
        )
        sums = sums + over_core(sums)
        sums = [sums] + over_y(sums)
        if sweep + 1 == ITERS:
            break
        update = call(update_kernel, gain_shape, 0, *sums, gains, misc)
        near = [over_z(update, d) for d in (1, 2, 3)]
        old = gains
        gains, m, code = call(
            next_kernel,
            (gain_shape, m_shape, code_shape),
            0,
            coef,
            update,
            *near,
            *[over_core(value) for value in near],
            misc,
            *static,
        )
        changes = call(
            functools.partial(change_kernel, sweep),
            jax.ShapeDtypeStruct((2, 128), F32),
            0,
            gains,
            old,
            misc,
            changes,
        )
    last = call(
        last_update_kernel, jax.ShapeDtypeStruct((40, 128), F32), 0, *sums, gains, misc, changes
    )
    near = [over_z(last, d) for d in (1, 2, 3, 4)]
    out_gains, part = call(
        finish_kernel,
        (jax.ShapeDtypeStruct((2, 2, 64), F32), jax.ShapeDtypeStruct((8, 128), F32)),
        0,
        final_coef,
        weight,
        last,
        *near,
        *[over_core(value) for value in near[0:3]],
        scratch=[pltpu.VMEM((8, 24, 128), F32), pltpu.VMEM((16, 128), F32)],
    )
    step_change = call(
        ratio_kernel, jax.ShapeDtypeStruct((2, ITERS), F32), 0, part, *over_x(part)
    )
    return out_gains, step_change


def solution(mesh):
    placed = (
        P(None, None, ("row", "col"), "chan"),
        P("chan", None, ("row", "col"), None),
        P("chan", None, ("row", "col")),
        P(("row", "col")),
        P(),
    )
    return jax.shard_map(
        shards,
        mesh=mesh,
        in_specs=placed,
        out_specs=(P("chan", None, ("row", "col")), P("chan", None)),
        check_vma=False,
    )
```

```python
import functools

import jax
import jax.numpy as jnp
from jax import lax
from jax.experimental import pallas as pl
from jax.experimental.pallas import tpu as pltpu
from jax.sharding import PartitionSpec as P


ITERS = 4
F32 = jnp.float32
BF16 = jnp.bfloat16
NT = (((1,), (1,)), ((), ()))


def call(kernel, out_shape, smem_count, *operands, scratch=()):
    in_specs = [pl.BlockSpec(memory_space=pltpu.SMEM)] * smem_count + [
        pl.BlockSpec(memory_space=pltpu.VMEM)
    ] * (len(operands) - smem_count)
    return pl.pallas_call(
        kernel,
        out_shape=out_shape,
        in_specs=in_specs,
        out_specs=jax.tree.map(lambda _: pl.BlockSpec(memory_space=pltpu.VMEM), out_shape),
        scratch_shapes=scratch,
        compiler_params=pltpu.CompilerParams(vmem_limit_bytes=24 * 1024 * 1024),
    )(*operands)


def lanes_merge(first, second):
    lane = lax.broadcasted_iota(jnp.int32, first.shape, first.ndim - 1)
    left = lane < 64
    low = jnp.where(left, first, pltpu.roll(second, 64, first.ndim - 1))
    high = jnp.where(left, pltpu.roll(first, 64, first.ndim - 1), second)
    return low, high


def turn_kernel(volt_ref, keep_ref, send_ref):
    core = lax.axis_index("col") % 2
    for chan in range(volt_ref.shape[0]):
        for ref, half in ((keep_ref, core), (send_ref, 1 - core)):
            block = volt_ref[chan, :, pl.ds(pl.multiple_of(half * 128, 128), 128)]
            ref[chan] = block.T


def place():
    return lax.axis_index("col") % 2, lax.axis_index("chan"), lax.axis_index("row")


def partner(z, core, distance):
    if distance == 4:
        return (z + 4) % 8
    group = z // 2 if distance == 2 else z
    return (z + distance * (1 - 2 * ((group + core) % 2)) + 8) % 8


def pack_kernel(keep_ref, recv_ref, s0, s1, s2, s3, out_ref):
    core, y_id, _ = place()
    flip = jnp.full((128, 128), core, jnp.int32) == 1
    for chan in range(keep_ref.shape[0]):
        own = keep_ref[chan].astype(F32)
        other = recv_ref[chan].astype(F32)
        low, high = lanes_merge(jnp.where(flip, other, own), jnp.where(flip, own, other))
        out_ref[chan, 0:128, :] = low.astype(BF16)
        out_ref[chan, 128:256, :] = high.astype(BF16)
    for step, ref in enumerate((s0, s1, s2, s3)):
        owner = lax.rem(y_id + 4 - step, 4)
        for b in range(2):
            out_ref[2 * owner + b, 256:400, :] = ref[b]


def lay_kernel(
    big_ref, other_ref, nat_ref, yr_ref, yi_ref, misc_ref, gain_ref, m_ref, code_ref
):
    core, y_id, _ = place()
    block = 2 * y_id + core
    flip = jnp.full((1, 128), core, jnp.int32) == 1
    for z in range(8):
        mine = pl.ds(pl.multiple_of(z * 128 + core * 64, 64), 64)
        theirs = pl.ds(pl.multiple_of(z * 128 + (1 - core) * 64, 64), 64)
        nat_ref[mine, 0:128] = big_ref[z, 256:320, :]
        nat_ref[mine, 128:256] = big_ref[z, 320:384, :]
        nat_ref[theirs, 0:128] = other_ref[z, 0:64, :]
        nat_ref[theirs, 128:256] = other_ref[z, 64:128, :]
        lanes = slice(z * 128, z * 128 + 128)
        x_re, x_im = big_ref[z, 0:128, :], big_ref[z, 128:256, :]
        yr_ref[0:128, lanes] = x_re
        yi_ref[0:128, lanes] = x_im
        own = big_ref[z, 384:400, :].astype(F32)
        other = other_ref[z, 128:144, :].astype(F32)
        own_gain = own[0:1] + own[1:2] + own[2:3]
        other_gain = other[0:1] + other[1:2] + other[2:3]
        gain_re, gain_im = lanes_merge(
            jnp.where(flip, other_gain, own_gain), jnp.where(flip, own_gain, other_gain)
        )
        weight, _ = lanes_merge(
            jnp.where(flip, other[3:4], own[3:4]), jnp.where(flip, own[3:4], other[3:4])
        )
        misc_ref[0:1, lanes] = gain_re
        misc_ref[1:2, lanes] = gain_im
        misc_ref[2:3, lanes] = weight
    nat = nat_ref[...]
    row = lax.broadcasted_iota(jnp.int32, (16, 128), 0) + block * 16
    pick = (row == lax.broadcasted_iota(jnp.int32, (16, 128), 1)).astype(BF16)
    yr_ref[128:144, :] = lax.dot_general(
        pick, nat[:, 0:128], NT, preferred_element_type=F32
    ).astype(BF16)
    yi_ref[128:144, :] = lax.dot_general(
        pick, nat[:, 128:256], NT, preferred_element_type=F32
    ).astype(BF16)
    gain_re, gain_im, weight = misc_ref[0:1], misc_ref[1:2], misc_ref[2:3]
    gain_ref[0:1] = gain_re
    gain_ref[1:2] = gain_im
    spread(gain_re, gain_im, weight, nat_ref, yr_ref, yi_ref, m_ref, code_ref)


def split(value):
    hi = value.astype(BF16)
    return hi, (value - hi.astype(F32)).astype(BF16)


def power_kernel(nat_ref, yr_ref, yi_ref, misc_ref, out_ref, weight_ref):
    wide = nat_ref[...].astype(F32)
    square = wide * wide
    hi = square.astype(BF16)
    lo = (square - hi.astype(F32)).astype(BF16)
    ones = jnp.ones((16, 256), BF16)
    alpha = lax.dot_general(ones, hi, NT, preferred_element_type=F32) + lax.dot_general(
        ones, lo, NT, preferred_element_type=F32
    )
    out_ref[0:1] = alpha[0:1]
    x_re, x_im = yr_ref[0:128].astype(F32), yi_ref[0:128].astype(F32)
    out_ref[1:2] = jnp.sum(x_re * x_re + x_im * x_im, axis=0, keepdims=True)
    for z in range(8):
        weight_ref[z : z + 1, :] = misc_ref[2:3, z * 128 : z * 128 + 128]


SPAN = 83.0
BLOCKS = ((0, 128), (128, 144))


def encode(m_ref, code_ref):
    scales = []
    for start, end in BLOCKS:
        value = m_ref[start:end, :]
        size = jnp.abs(value)
        scale = jnp.maximum(jnp.max(size, axis=0, keepdims=True) * 1.01, 1e-30)
        scale = scale.astype(BF16).astype(F32)
        code = jnp.exp(size * (SPAN / scale))
        code_ref[start:end, :] = jnp.where(value < 0, -code, code).astype(BF16)
        scales.append(scale)
    scales.append(jnp.zeros((14, 256), F32))
    code_ref[144:160, :] = jnp.concatenate(scales, axis=0).astype(BF16)


def decode(code_ref):
    scales = code_ref[144:160, :].astype(F32)
    parts = []
    for index, (start, end) in enumerate(BLOCKS):
        code = code_ref[start:end, :].astype(F32)
        size = jnp.log(jnp.abs(code)) * (scales[index : index + 1] * (1 / SPAN))
        parts.append(jnp.where(code < 0, -size, size))
    return jnp.concatenate(parts, axis=0)


def spread(gain_re, gain_im, weight, nat_ref, yr_ref, yi_ref, m_ref, code_ref):
    w_re = weight * gain_re
    w_im = weight * gain_im
    w_pow = weight * (gain_re * gain_re + gain_im * gain_im)
    total = None
    for start in range(0, nat_ref.shape[0], 256):
        lanes = slice(start, start + 256)
        row = lax.broadcasted_iota(jnp.int32, (144, 256), 0) < 128
        c_re = jnp.where(row, w_re[:, lanes], w_pow[:, lanes])
        c_im = jnp.where(row, w_im[:, lanes], 0.0)
        y_re = yr_ref[:, lanes].astype(F32)
        y_im = yi_ref[:, lanes].astype(F32)
        re_hi, re_lo = split(y_re * c_re + y_im * c_im)
        im_hi, im_lo = split(y_re * c_im - y_im * c_re)
        left = jnp.concatenate([re_hi, re_lo, im_hi, im_lo], axis=0)
        part = jnp.dot(left, nat_ref[lanes, :], preferred_element_type=F32)
        total = part if total is None else total + part
    re = total[0:144] + total[144:288]
    im = total[288:432] + total[432:576]
    m_ref[:, 0:128] = re[:, 0:128] - im[:, 128:256]
    m_ref[:, 128:256] = re[:, 128:256] + im[:, 0:128]
    encode(m_ref, code_ref)


def weight_of(near_ref, chan, other):
    value = jnp.where(chan == other, 0.5, 0.0)
    value = value + jnp.where(near_ref[chan, 0] == other, 0.25, 0.0)
    return value + jnp.where(near_ref[chan, 1] == other, 0.25, 0.0)


def sources_of(z, core):
    return [z] + [partner(z, core, d) for d in (1, 2, 3, 4)] + [partner(z, 1 - core, d) for d in (1, 2, 3)]


def coef_kernel(near_ref, power_ref, coef_ref, final_ref, out_ref):
    out_ref[...] = power_ref[...]
    core, y_id, z_id = place()
    for index, other in enumerate(sources_of(z_id, core)):
        coef_ref[index : index + 1, :] = jnp.full((1, 1024), weight_of(near_ref, z_id, other), F32)
        for b in range(2):
            value = weight_of(near_ref, 2 * y_id + b, other)
            final_ref[b, index : index + 1, :] = jnp.full((1, 128), value, F32)


def next_kernel(coef_ref, u0, u1, u2, u3, v1, v2, v3, misc_ref, nat_ref, yr_ref, yi_ref, gain_ref, m_ref, code_ref):
    smooth = coef_ref[0:1] * u0[...]
    for index, ref in ((1, u1), (2, u2), (3, u3), (5, v1), (6, v2), (7, v3)):
        smooth = smooth + coef_ref[index : index + 1] * ref[...]
    gain_ref[...] = smooth
    spread(smooth[0:1], smooth[1:2], misc_ref[2:3], nat_ref, yr_ref, yi_ref, m_ref, code_ref)


def change_kernel(sweep, new_ref, old_ref, misc_ref, changes_ref, out_ref):
    diff = new_ref[...] - old_ref[...]
    lane = lax.broadcasted_iota(jnp.int32, (1, 128), 1)
    for row, value in ((0, diff), (1, new_ref[...])):
        total = jnp.sum(misc_ref[2:3] * value * value, axis=0, keepdims=True)
        total = jnp.sum(total, axis=1, keepdims=True)
        out_ref[row : row + 1] = jnp.where(lane == sweep, total, changes_ref[row : row + 1])


def collect_kernel(m0, m1, m2, m3, gain_ref, misc_ref, power_ref, nat_ref, yr_ref, yi_ref, out_ref):
    total = (m0[...] + decode(m1)) + (decode(m2) + decode(m3))
    re, im = total[:, 0:128], total[:, 128:256]
    a_hi, a_lo = split(total)
    b_hi, b_lo = split(jnp.concatenate([im, -re], axis=1))
    left = jnp.concatenate([a_hi, a_lo, b_hi, b_lo], axis=0)
    for start in range(0, nat_ref.shape[0], 256):
        lanes = slice(start, start + 256)
        part = lax.dot_general(left, nat_ref[lanes, :], NT, preferred_element_type=F32)
        z_re = part[0:144] + part[144:288]
        z_im = part[288:432] + part[432:576]
        y_re = yr_ref[:, lanes].astype(F32)
        y_im = yi_ref[:, lanes].astype(F32)
        real = y_re * z_re - y_im * z_im
        imag = y_re * z_im + y_im * z_re
        num_re = jnp.sum(real[0:128], axis=0, keepdims=True)
        num_im = jnp.sum(imag[0:128], axis=0, keepdims=True)
        den = jnp.sum(real[128:144], axis=0, keepdims=True)
        g_re, g_im = gain_ref[0:1, lanes], gain_ref[1:2, lanes]
        weight = misc_ref[2:3, lanes]
        alpha, power = power_ref[0:1, lanes], power_ref[1:2, lanes]
        own = alpha * power * weight
        out_ref[0:1, lanes] = num_re - own * g_re
        out_ref[1:2, lanes] = num_im - own * g_im
        out_ref[2:3, lanes] = den - 0.125 * alpha * alpha * weight * (g_re * g_re + g_im * g_im)
        out_ref[3:4, lanes] = jnp.zeros_like(den)


def updated(n0, n1, n2, n3, gain_ref, misc_ref):
    total = (n0[...] + n1[...]) + (n2[...] + n3[...])
    g_re, g_im = gain_ref[0:1], gain_ref[1:2]
    live = misc_ref[2:3] > 0.5
    den = total[2:3]
    u_re = jnp.where(live, 0.5 * (0.125 * total[0:1] / den + g_re), g_re)
    u_im = jnp.where(live, 0.5 * (0.125 * total[1:2] / den + g_im), g_im)
    return u_re, u_im


def update_kernel(n0, n1, n2, n3, gain_ref, misc_ref, out_ref):
    u_re, u_im = updated(n0, n1, n2, n3, gain_ref, misc_ref)
    out_ref[0:1] = u_re
    out_ref[1:2] = u_im


def last_update_kernel(n0, n1, n2, n3, gain_ref, misc_ref, changes_ref, out_ref):
    u_re, u_im = updated(n0, n1, n2, n3, gain_ref, misc_ref)
    for index, value in enumerate((u_re, u_im, gain_ref[0:1], gain_ref[1:2])):
        for z in range(8):
            row = index * 8 + z
            out_ref[row : row + 1, :] = value[:, z * 128 : z * 128 + 128]
    out_ref[32:34, :] = changes_ref[...]
    out_ref[34:40, :] = jnp.zeros((6, 128), F32)


def finish_kernel(coef_ref, weight_ref, *refs):
    pieces, (smooth_ref, sums_ref, all_ref) = refs[0:8], refs[8:]
    core, y_id, z_id = place()
    for other, ref in zip(sources_of(z_id, core), pieces):
        all_ref[other] = ref[16:40, :]
    weight = weight_ref[...]
    lane = lax.broadcasted_iota(jnp.int32, (1, 128), 1)
    for b in range(2):
        smooth = coef_ref[b, 0:1] * pieces[0][0:16, :]
        for index in range(1, 8):
            smooth = smooth + coef_ref[b, index : index + 1] * pieces[index][0:16, :]
        smooth_ref[b] = smooth
        past = all_ref[2 * y_id + b]
        diff = smooth - past[0:16]
        for index, value in enumerate((diff, smooth)):
            total = weight * (value[0:8] * value[0:8] + value[8:16] * value[8:16])
            total = jnp.sum(jnp.sum(total, axis=0, keepdims=True), axis=1, keepdims=True)
            row = 2 * index + b
            sums_ref[row : row + 1, :] = jnp.where(
                lane == ITERS - 1, total, past[16 + index : 17 + index]
            )
    sums_ref[4:8, :] = jnp.zeros((4, 128), F32)


def gains_kernel(smooth_ref, gains_ref):
    core, _, z_id = place()
    flip = jnp.full((1, 128), core, jnp.int32) == 1
    for b in range(2):
        for part in range(2):
            row = smooth_ref[b, pl.ds(part * 8 + z_id, 1), :]
            row = jnp.where(flip, pltpu.roll(row, 64, 1), row)
            gains_ref[b, part : part + 1, :] = row[:, 0:64]


def ratio_kernel(p0, p1, p2, p3, out_ref):
    total = (p0[...] + p1[...]) + (p2[...] + p3[...])
    out_ref[...] = total[0:2, 0:ITERS] / (total[2:4, 0:ITERS] + 1e-06)


def shards(voltages, sources, initial_gains, flags, neighbours):
    def over_core(value):
        return lax.ppermute(value, "col", [(i, i ^ 1) for i in range(8)])

    def over_x(value):
        return [
            lax.ppermute(value, "col", [(i, (i + 2 * d) % 8) for i in range(8)]) for d in (2, 1, 3)
        ]

    def over_y(value):
        return [lax.ppermute(value, "chan", [(i, (i + d) % 4) for i in range(4)]) for d in (1, 2, 3)]

    def over_z(value, distance):
        pairs = [(z * 8 + c, partner(z, c % 2, distance) * 8 + c) for z in range(8) for c in range(8)]
        return lax.ppermute(value, ("row", "col"), pairs)

    gain = initial_gains.reshape(2, 128)
    hi = lax.reduce_precision(gain, 8, 7)
    mid = lax.reduce_precision(gain - hi, 8, 7)
    weight = jnp.tile(jnp.repeat(1.0 - flags.astype(F32), 2), 2)
    extra = jnp.stack([hi, mid, gain - hi - mid, jnp.broadcast_to(weight, (2, 128))], axis=1)
    extra = jnp.concatenate([extra, jnp.zeros((2, 12, 128), F32)], axis=1).astype(BF16)
    sky = jnp.concatenate([sources.reshape(2, 128, 128), extra], axis=1)
    sky_all = [sky] + over_y(sky)

    half = jax.ShapeDtypeStruct((8, 128, 128), BF16)
    keep, send = call(turn_kernel, (half, half), 0, voltages.reshape(8, 128, 256))
    recv = over_core(send)
    packed = call(
        pack_kernel, jax.ShapeDtypeStruct((8, 400, 128), BF16), 0, keep, recv, *sky_all
    )
    big = lax.all_to_all(packed, "row", split_axis=0, concat_axis=0, tiled=True)
    gain_shape = jax.ShapeDtypeStruct((2, 1024), F32)
    m_shape = jax.ShapeDtypeStruct((144, 256), F32)
    code_shape = jax.ShapeDtypeStruct((160, 256), BF16)
    nat, y_re, y_im, misc, gains, m, code = call(
        lay_kernel,
        (
            jax.ShapeDtypeStruct((1024, 256), BF16),
            jax.ShapeDtypeStruct((144, 1024), BF16),
            jax.ShapeDtypeStruct((144, 1024), BF16),
            jax.ShapeDtypeStruct((8, 1024), F32),
            gain_shape,
            m_shape,
            code_shape,
        ),
        0,
        big,
        over_core(big[:, 256:400]),
    )
    static = (nat, y_re, y_im)
    power, weight = call(
        power_kernel, (gain_shape, jax.ShapeDtypeStruct((8, 128), F32)), 0, *static, misc
    )
    coef, final_coef, power = call(
        coef_kernel,
        (jax.ShapeDtypeStruct((8, 1024), F32), jax.ShapeDtypeStruct((2, 8, 128), F32), gain_shape),
        1,
        neighbours,
        power,
    )
    changes = jnp.zeros((2, 128), F32)
    for sweep in range(ITERS):
        sums = call(
            collect_kernel,
            jax.ShapeDtypeStruct((4, 1024), F32),
            0,
            m,
            *over_x(code),
            gains,
            misc,
            power,
            *static,
        )
        sums = sums + over_core(sums)
        sums = [sums] + over_y(sums)
        if sweep + 1 == ITERS:
            break
        update = call(update_kernel, gain_shape, 0, *sums, gains, misc)
        by_distance = {d: over_z(update, d) for d in (3, 1, 2)}
        near = [by_distance[d] for d in (1, 2, 3)]
        old = gains
        gains, m, code = call(
            next_kernel,
            (gain_shape, m_shape, code_shape),
            0,
            coef,
            update,
            *near,
            *[over_core(value) for value in near],
            misc,
            *static,
        )
        changes = call(
            functools.partial(change_kernel, sweep),
            jax.ShapeDtypeStruct((2, 128), F32),
            0,
            gains,
            old,
            misc,
            changes,
        )
    last = call(
        last_update_kernel, jax.ShapeDtypeStruct((40, 128), F32), 0, *sums, gains, misc, changes
    )
    near = [over_z(last, d) for d in (1, 2, 3, 4)]
    smooth, part = call(
        finish_kernel,
        (jax.ShapeDtypeStruct((2, 16, 128), F32), jax.ShapeDtypeStruct((8, 128), F32)),
        0,
        final_coef,
        weight,
        last,
        *near,
        *[over_core(value) for value in near[0:3]],
        scratch=[pltpu.VMEM((8, 24, 128), F32)],
    )
    out_gains = call(gains_kernel, jax.ShapeDtypeStruct((2, 2, 64), F32), 0, smooth)
    step_change = call(
        ratio_kernel, jax.ShapeDtypeStruct((2, ITERS), F32), 0, part, *over_x(part)
    )
    return out_gains, step_change


def solution(mesh):
    placed = (
        P(None, None, ("row", "col"), "chan"),
        P("chan", None, ("row", "col"), None),
        P("chan", None, ("row", "col")),
        P(("row", "col")),
        P(),
    )
    return jax.shard_map(
        shards,
        mesh=mesh,
        in_specs=placed,
        out_specs=(P("chan", None, ("row", "col")), P("chan", None)),
        check_vma=False,
    )
```
